32 devices in a mesh: ctx: 16 (over z, y, core), mp: 2 (over x).
Axes of the slice: x: 2, y: 2, z: 4, core: 2. Of those that a mesh axis runs over, the one named last changes fastest.
Arguments:
- sublayer_input: bfloat16 [2048, 4096], P('ctx'), may hold values from -6 to 6
- rotated_queries: bfloat16 [2048, 8192], P('ctx', 'mp'), may hold values from -5 to 5
- rotated_keys: bfloat16 [2048, 1024], P('ctx', 'mp'), may hold values from -5 to 5
- output_grad: bfloat16 [2048, 8192], P('ctx', 'mp'), may hold values from -6 to 6
- value_weight: bfloat16 [4096, 1024], P(None, 'mp'), may hold values from -0.09375 to 0.09375
- segment_ids: int32 [2048], replicated, may hold values from 0 to 3, never falling along the last dimension, each value on 1 to 1536 neighbouring positions
- label_positions: int32 [128], replicated, may hold values from 0 to 2047
Outputs:
- query_grad: bfloat16 [2048, 8192], P('ctx', 'mp')
- key_grad: bfloat16 [2048, 1024], P('ctx', 'mp')
- input_grad: bfloat16 [2048, 4096], P('ctx', 'mp')
- value_weight_grad: bfloat16 [4096, 1024], P('ctx', 'mp')
The draws below stay inside these ranges and needn't reach their ends.
Inputs may be any that keep to these rules, and one draw needn't show every extreme that they name: `segment_ids`: ids never fall along the slab; one trace takes exactly 1536 positions. `label_positions`: a position may appear more than once.
All inputs are finite; a program needn't handle non-finite values.
Results may differ from the reference program's by a relative error of at most 0.017.
Values may be sent and summed in bfloat16 or wider, within the bound.
A program may use at most 64 MiB of HBM per device.

```python
import math
import jax
import jax.numpy as jnp
import numpy as np
from jax import lax

HEADS = 64
KV_HEADS = 8
HD = 128
D = 4096
DOCS = 4
LABELS = 128
TOKENS = 2048
LONGEST = 1536


def draw_rotated_queries(key, part):
    base = jax.random.truncated_normal(jax.random.fold_in(key, 21), -4.0, 4.0, (TOKENS, HEADS * HD), jnp.float32)
    return base.astype(jnp.bfloat16)


def draw_rotated_keys(key, part):
    base = jax.random.truncated_normal(jax.random.fold_in(key, 22), -4.0, 4.0, (TOKENS, KV_HEADS * HD), jnp.float32)
    return base.astype(jnp.bfloat16)


def place_ends(drawn, stream_key, least, top_value):
    index_at = [jax.random.randint(jax.random.fold_in(stream_key, axis), (), 0, length) for axis, length in enumerate(drawn.shape)]
    widest = drawn.shape.index(max(drawn.shape))
    next_to = index_at[:widest] + [(index_at[widest] + 1) % drawn.shape[widest]] + index_at[widest + 1:]
    return drawn.at[tuple(index_at)].set(least).at[tuple(next_to)].set(top_value)


def spiked(values, own_key, source, target, blocks, factor):
    def block_of(position):
        return (jnp.arange(values.shape[position]) // (values.shape[position] // blocks)).reshape((-1,) + (1,) * (values.ndim - 1 - position))

    one_side = jax.random.permutation(own_key, blocks)[block_of(target)]
    far = (block_of(target) + blocks // 2) % blocks
    return jnp.where((block_of(source) == one_side) | (block_of(source) == far), factor * values, values)


def block_scale(own_key, extent, cuts, smallest, high):
    gain, own = 1.0, jax.random.fold_in(own_key, 6)
    for axis_at, shards_of in cuts:
        heights = jnp.exp(jax.random.uniform(jax.random.fold_in(own, axis_at), (shards_of,), jnp.float32, smallest / len(cuts), high / len(cuts)))
        gain = gain * jnp.repeat(heights, extent[axis_at] // shards_of).reshape([-1 if axis == axis_at else 1 for axis in range(len(extent))])
    return gain


def profile(number_of, total, limit, skew):
    loads = [(1 << 20) // math.isqrt(grade ** skew) + 1 for grade in range(2, number_of + 1)]
    rest, holding = total - limit - (number_of - 1), [1] * (number_of - 1)
    while rest > 0:
        candidates = [i for i in range(number_of - 1) if holding[i] < limit]
        mass, remaining = sum([loads[i] for i in candidates]), rest
        for i in candidates:
            addition = min(limit - holding[i], max(1, remaining * loads[i] // mass), rest)
            holding[i] = holding[i] + addition
            rest = rest - addition
    return np.array([limit] + holding)


def uneven_parts(own_key, amount, total, reach, skew):
    if amount == 2:
        one = jax.random.randint(own_key, (), max(1, total - reach), min(reach, total - 1) + 1)
        return jnp.stack([one, total - one])
    sizes = jnp.asarray(profile(amount, total, reach, skew), jnp.int32)
    couples = (amount - 1) // 2
    source_of, receiver = sizes[1:1 + 2 * couples:2], sizes[2:2 + 2 * couples:2]
    slack = jnp.minimum(source_of - 1, reach - receiver)
    shifted = jax.random.randint(jax.random.fold_in(own_key, 1), (couples,), 0, 1 << 20) % (slack + 1)
    sizes = sizes.at[1:1 + 2 * couples:2].set(source_of - shifted).at[2:2 + 2 * couples:2].set(receiver + shifted)
    return sizes[jax.random.permutation(jax.random.fold_in(own_key, 2), amount)]


def centred(rng, dims, spread, reach, shards=(), kind=jnp.bfloat16):
    drawn = spread * jax.random.normal(rng, dims, jnp.float32)
    if shards:
        drawn = drawn * block_scale(rng, dims, shards, -0.22, 0.18)
    return jnp.clip(drawn, -reach, reach).astype(kind)


def bell_draw_with(key, shape, width, bound, split, heavy, held_as=jnp.bfloat16):
    drawn = width * jax.random.normal(key, shape, jnp.float32)
    if split:
        drawn = drawn * block_scale(key, shape, split, -0.22, 0.18)
    return jnp.clip(spiked(drawn, jax.random.fold_in(key, 3), *heavy), -bound, bound).astype(held_as)


def setup_inputs(seed: int = 0) -> dict:
    key_of = jax.random.split(jax.random.key(seed), 8)
    return {
        "sublayer_input": bell_draw_with(key_of[0], (TOKENS, D), 1.0, 6.0, ((0, 16),), (0, 1, 16, 2.0)),
        "rotated_queries": draw_rotated_queries(jax.random.fold_in(key_of[7], 71), 0),
        "rotated_keys": draw_rotated_keys(jax.random.fold_in(key_of[7], 71), 0),
        "output_grad": centred(key_of[3], (TOKENS, HEADS * HD), 1.0, 6.0, ((0, 16), (1, 2))),
        "value_weight": centred(key_of[4], (D, KV_HEADS * HD), D ** -0.5, 0.09375, ((1, 2),)),
        "segment_ids": jnp.searchsorted(jnp.cumsum(uneven_parts(key_of[5], DOCS, TOKENS, LONGEST, 2)), jnp.arange(TOKENS), side="right").astype(jnp.int32),
        "label_positions": place_ends(jax.random.randint(key_of[6], (LABELS,), 0, TOKENS), jax.random.fold_in(key_of[6], 1), 0, TOKENS - 1).astype(jnp.int32),
    }


NEGATIVE = -1.0e30


def reference(sublayer_input, rotated_queries, rotated_keys, output_grad, value_weight, segment_ids, label_positions):
    total_rows = sublayer_input.shape[0]
    group_size = HEADS // KV_HEADS
    score_scale = HD ** -0.5
    positions = jnp.arange(total_rows, dtype=jnp.int32)
    labelled = jnp.any(positions[:, None] == label_positions[None, :], axis=1)
    loss_weight = jnp.where(labelled, 4.0, 1.0).astype(jnp.float32)
    weighted = (output_grad.astype(jnp.float32) * loss_weight[:, None]).astype(jnp.bfloat16)
    values = jnp.dot(sublayer_input, value_weight, preferred_element_type=jnp.float32).astype(jnp.bfloat16)
    query_heads = rotated_queries.reshape(total_rows, KV_HEADS, group_size, HD).transpose(1, 2, 0, 3)
    grad_heads = weighted.reshape(total_rows, KV_HEADS, group_size, HD).transpose(1, 2, 0, 3)
    key_heads = rotated_keys.reshape(total_rows, KV_HEADS, HD).transpose(1, 0, 2)
    value_heads = values.reshape(total_rows, KV_HEADS, HD).transpose(1, 0, 2)
    query_block = 512 if total_rows % 512 == 0 else total_rows
    block_count = total_rows // query_block

    def per_head(operands):
        query_one, grad_one, key_one, value_one = operands
        key_full = key_one.astype(jnp.float32)
        value_full = value_one.astype(jnp.float32)

        def per_block(carry, block_index):
            key_sum, value_sum = carry
            block_start = (block_index * query_block).astype(jnp.int32)
            query_part = lax.dynamic_slice_in_dim(query_one, block_start, query_block, 1).astype(jnp.float32)
            grad_part = lax.dynamic_slice_in_dim(grad_one, block_start, query_block, 1).astype(jnp.float32)
            row_positions = block_start + jnp.arange(query_block, dtype=jnp.int32)
            row_segments = lax.dynamic_slice_in_dim(segment_ids, block_start, query_block)
            allowed = (row_segments[:, None] == segment_ids[None, :]) & (row_positions[:, None] >= positions[None, :])
            allowed = allowed[None, :, :]
            scores = jnp.einsum("gqd,kd->gqk", query_part, key_full) * score_scale
            masked = jnp.where(allowed, scores, NEGATIVE)
            row_top = jnp.max(masked, axis=-1, keepdims=True)
            exp_total = jnp.sum(jnp.where(allowed, jnp.exp(masked - row_top), 0.0), axis=-1, keepdims=True)
            log_total = row_top + jnp.log(exp_total)
            probabilities = jnp.where(allowed, jnp.exp(masked - log_total), 0.0)
            grad_probs = jnp.einsum("gqd,kd->gqk", grad_part, value_full)
            delta = jnp.sum(probabilities * grad_probs, axis=-1, keepdims=True)
            probs_low = lax.optimization_barrier(probabilities.astype(jnp.bfloat16))
            grad_scores = lax.optimization_barrier((probabilities * (grad_probs - delta) * score_scale).astype(jnp.bfloat16))
            probs_wide = probs_low.astype(jnp.float32)
            scores_wide = grad_scores.astype(jnp.float32)
            query_part_grad = jnp.einsum("gqk,kd->gqd", scores_wide, key_full).astype(jnp.bfloat16)
            key_sum = key_sum + jnp.einsum("gqk,gqd->kd", scores_wide, query_part)
            value_sum = value_sum + jnp.einsum("gqk,gqd->kd", probs_wide, grad_part)
            return (key_sum, value_sum), query_part_grad

        start_sums = (jnp.zeros((total_rows, HD), jnp.float32), jnp.zeros((total_rows, HD), jnp.float32))
        (key_sum, value_sum), query_blocks = lax.scan(per_block, start_sums, jnp.arange(block_count, dtype=jnp.int32))
        return key_sum, value_sum, query_blocks

    key_sums, value_sums, query_blocks = lax.map(per_head, (query_heads, grad_heads, key_heads, value_heads))
    query_grad = query_blocks.transpose(1, 3, 0, 2, 4).reshape(total_rows, HEADS * HD)
    key_grad = key_sums.transpose(1, 0, 2).reshape(total_rows, KV_HEADS * HD).astype(jnp.bfloat16)
    value_grad = value_sums.transpose(1, 0, 2).reshape(total_rows, KV_HEADS * HD).astype(jnp.bfloat16)
    input_grad = jnp.dot(value_grad, value_weight.T, preferred_element_type=jnp.float32).astype(jnp.bfloat16)
    value_weight_grad = jnp.dot(sublayer_input.T, value_grad, preferred_element_type=jnp.float32).astype(jnp.bfloat16)
    return query_grad, key_grad, input_grad, value_weight_grad
```

```python
import functools

import jax
import jax.numpy as jnp
from jax import lax
from jax.experimental import pallas as pl
from jax.experimental.pallas import tpu as pltpu
from jax.sharding import PartitionSpec as P

HEADS = 64
KV_HEADS = 8
HD = 128
GROUP = HEADS // KV_HEADS
SCALE = HD ** (-0.5)
LOG2E = 1.4426950408889634
NEGATIVE = -1e30
MESH = pl.DeviceIdType.MESH
SLAB = 4
CORE = 1
SIDE = 2
BF = jnp.bfloat16
F32 = jnp.float32
VMEM_LIMIT = 56 * 1024 * 1024


def remote(src, dst, send, recv, axis, index):
    return pltpu.make_async_remote_copy(
        src_ref=src,
        dst_ref=dst,
        send_sem=send,
        recv_sem=recv,
        device_id={axis: index},
        device_id_type=MESH,
    )


def greet(me, slab, slabs, mp_count):
    barrier = pltpu.get_barrier_semaphore()

    def signal(axis, index):
        pl.semaphore_signal(barrier, inc=1, device_id={axis: index}, device_id_type=MESH)

    pos = lax.rem(me, SLAB)
    base = me - pos
    signal("ctx", base + flip(pos, CORE))
    signal("ctx", base + flip(pos, SIDE))

    @pl.when(slab > 0)
    def _():
        signal("ctx", me - SLAB)

    @pl.when(slab < slabs - 1)
    def _():
        signal("ctx", me + SLAB)

    mine = lax.axis_index("mp")
    for d in range(1, mp_count):
        signal("mp", lax.rem(mine + d, mp_count))
    neighbours = jnp.minimum(slab, 1) + jnp.minimum(slabs - 1 - slab, 1)
    pl.semaphore_wait(barrier, neighbours + (2 + mp_count - 1))


def flip(pos, bit):
    if bit == CORE:
        return pos + 1 - 2 * lax.rem(pos, 2)
    return lax.rem(pos + 2, SLAB)


def gather_kernel(slabs, k_ref, v_ref, ok_ref, ov_ref, recv, send):
    me = lax.axis_index("ctx")
    slab = me // SLAB
    pos = lax.rem(me, SLAB)
    base = me - pos
    core_pos, side_pos = flip(pos, CORE), flip(pos, SIDE)
    both_pos = flip(side_pos, CORE)
    outs = (ok_ref, ov_ref)
    greet(me, slab, slabs, 1)
    ok_ref[me] = k_ref[...]
    ov_ref[me] = v_ref[...]

    def copy(half, dest, block):
        target = (me + SLAB, base + side_pos, base + core_pos)[dest]
        ref = outs[half].at[block]
        return remote(ref, ref, send.at[half, dest, block], recv.at[half, block], "ctx", target)

    def cross(s):
        block = s * SLAB + side_pos
        for half in range(2):
            copy(half, 1, block).wait_recv()
            copy(half, 2, block).start()

    def step(k, _):
        s = slab - k
        block = s * SLAB + pos
        for half in range(2):

            @pl.when(k > 0)
            def _():
                copy(half, 0, block).wait_recv()

            @pl.when(slab < slabs - 1)
            def _():
                copy(half, 0, block).start()

            copy(half, 1, block).start()
            copy(half, 2, block).start()

        @pl.when(k > 0)
        def _():
            cross(s + 1)

        return 0

    lax.fori_loop(0, slab + 1, step, 0)
    cross(0)

    def finish(s, _):
        for half in range(2):
            copy(half, 2, s * SLAB + core_pos).wait_recv()
            copy(half, 2, s * SLAB + both_pos).wait_recv()

            @pl.when(slab < slabs - 1)
            def _():
                copy(half, 0, s * SLAB + pos).wait_send()

            copy(half, 1, s * SLAB + pos).wait_send()
            copy(half, 2, s * SLAB + pos).wait_send()
            copy(half, 2, s * SLAB + side_pos).wait_send()
        return 0

    lax.fori_loop(0, slab + 1, finish, 0)


def gather_blocks(keys, values, count):
    rows, width = keys.shape
    shape = jax.ShapeDtypeStruct((count, rows, width), BF)
    vmem = pl.BlockSpec(memory_space=pltpu.VMEM)
    moved = count * rows * width * 4
    return pl.pallas_call(
        functools.partial(gather_kernel, count // SLAB),
        out_shape=(shape, shape),
        in_specs=[vmem, vmem],
        out_specs=(vmem, vmem),
        scratch_shapes=[
            pltpu.SemaphoreType.DMA((2, count)),
            pltpu.SemaphoreType.DMA((2, 3, count)),
        ],
        compiler_params=pltpu.CompilerParams(
            collective_id=0, has_side_effects=True, vmem_limit_bytes=VMEM_LIMIT
        ),
        cost_estimate=pl.CostEstimate(flops=0, bytes_accessed=moved, transcendentals=0),
        name="gather_keys_values",
    )(keys, values)


def reduce_kernel(
    slabs, mp_count, pk_ref, pv_ref, dk_ref, all_ref, pair_ref,
    rc, ry, rz, sy, sz, rc_sem, ry_sem, rz_sem, sc_sem, sy_sem, sz_sem,
    ag_recv, ag_send, mp_recv, mp_send,
):
    me = lax.axis_index("ctx")
    mine = lax.axis_index("mp")
    slab = me // SLAB
    pos = lax.rem(me, SLAB)
    base = me - pos
    core_pos, side_pos = flip(pos, CORE), flip(pos, SIDE)
    both_pos = flip(side_pos, CORE)
    parts = (pv_ref, pk_ref)
    greet(me, slab, slabs, mp_count)

    def core_copy(half, which, s):
        block = s * SLAB + (core_pos, both_pos)[which]
        return remote(
            parts[half].at[block], rc.at[half, which, s],
            sc_sem.at[half, which, s], rc_sem.at[half, which, s], "ctx", base + core_pos,
        )

    def side_copy(half, s):
        return remote(
            sy.at[half, s], ry.at[half, s], sy_sem.at[half, s], ry_sem.at[half, s],
            "ctx", base + side_pos,
        )

    def down_copy(half, s):
        return remote(
            sz.at[half, s], rz.at[half, s], sz_sem.at[half, s], rz_sem.at[half, s],
            "ctx", me - SLAB,
        )

    for half in range(2):

        def start_core(s, _):
            core_copy(half, 1, s).start()
            core_copy(half, 0, s).start()
            return 0

        lax.fori_loop(0, slab + 1, start_core, 0)

    for half in range(2):

        def start_side(s, _):
            core_copy(half, 1, s).wait_recv()
            total = parts[half][s * SLAB + side_pos].astype(F32) + rc[half, 1, s].astype(F32)
            sy[half, s] = total.astype(BF)
            side_copy(half, s).start()
            return 0

        lax.fori_loop(0, slab + 1, start_side, 0)

    def own_total(half, s):
        core_copy(half, 0, s).wait_recv()
        total = parts[half][s * SLAB + pos].astype(F32) + rc[half, 0, s].astype(F32)
        side_copy(half, s).wait_recv()
        return total + ry[half, s].astype(F32)

    def reduce_half(half, out, index):
        def one(s, _):
            total = own_total(half, s)

            @pl.when(slab < slabs - 1)
            def _():
                down_copy(half, s).wait_recv()
                full = total + rz[half, s].astype(F32)

                @pl.when(s < slab)
                def _():
                    sz[half, s] = full.astype(BF)
                    down_copy(half, s).start()

                @pl.when(s == slab)
                def _():
                    store(full)

            @pl.when(slab == slabs - 1)
            def _():
                @pl.when(s < slab)
                def _():
                    sz[half, s] = total.astype(BF)
                    down_copy(half, s).start()

                @pl.when(s == slab)
                def _():
                    store(total)

            return 0

        def store(total):
            if index is None:
                out[...] = total.astype(BF)
            else:
                out[index] = total.astype(BF)

        lax.fori_loop(0, slab + 1, one, 0)

    def ag_copy(dest, block):
        target = (me + SLAB, me - SLAB, base + side_pos, base + core_pos)[dest]
        ref = all_ref.at[block]
        return remote(ref, ref, ag_send.at[dest, block], ag_recv.at[block], "ctx", target)

    def mp_copy(peer):
        return remote(
            all_ref.at[me], pair_ref.at[mine], mp_send.at[peer], mp_recv.at[mine], "mp", peer
        )

    def mp_arrival(peer):
        return remote(
            all_ref.at[me], pair_ref.at[peer], mp_send.at[peer], mp_recv.at[peer], "mp", peer
        )

    reduce_half(0, all_ref, me)
    for d in range(1, mp_count):
        mp_copy(lax.rem(mine + d, mp_count)).start()

    @pl.when(slab < slabs - 1)
    def _():
        ag_copy(0, me).start()

    @pl.when(slab > 0)
    def _():
        ag_copy(1, me).start()

    ag_copy(2, me).start()
    ag_copy(3, me).start()
    pair_ref[mine] = all_ref[me]
    reduce_half(1, dk_ref, None)

    def cross(s):
        block = s * SLAB + side_pos
        ag_copy(2, block).wait_recv()
        ag_copy(3, block).start()

    def spread(k, _):
        low, high = slab - k, slab + k

        @pl.when(low >= 0)
        def _():
            block = low * SLAB + pos
            ag_copy(0, block).wait_recv()

            @pl.when(slab < slabs - 1)
            def _():
                ag_copy(0, block).start()

            ag_copy(2, block).start()
            ag_copy(3, block).start()

        @pl.when(high < slabs)
        def _():
            block = high * SLAB + pos
            ag_copy(0, block).wait_recv()

            @pl.when(slab > 0)
            def _():
                ag_copy(1, block).start()

            ag_copy(2, block).start()
            ag_copy(3, block).start()

        return 0

    lax.fori_loop(1, slabs, spread, 0)

    def cross_all(s, _):
        cross(s)
        return 0

    lax.fori_loop(0, slabs, cross_all, 0)

    def finish_all(s, _):
        ag_copy(3, s * SLAB + core_pos).wait_recv()
        ag_copy(3, s * SLAB + both_pos).wait_recv()
        own = s * SLAB + pos

        @pl.when((s <= slab) & (slab < slabs - 1))
        def _():
            ag_copy(0, own).wait_send()

        @pl.when((s >= slab) & (slab > 0))
        def _():
            ag_copy(1, own).wait_send()

        ag_copy(2, own).wait_send()
        ag_copy(3, own).wait_send()
        ag_copy(3, s * SLAB + side_pos).wait_send()
        return 0

    lax.fori_loop(0, slabs, finish_all, 0)
    for d in range(1, mp_count):
        peer = lax.rem(mine + d, mp_count)
        mp_arrival(peer).wait_recv()
        mp_arrival(peer).wait_send()
    for half in range(2):

        def finish(s, _):
            core_copy(half, 0, s).wait_send()
            core_copy(half, 1, s).wait_send()
            side_copy(half, s).wait_send()

            @pl.when(s < slab)
            def _():
                down_copy(half, s).wait_send()

            return 0

        lax.fori_loop(0, slab + 1, finish, 0)


def reduce_blocks(key_parts, value_parts, mp_count):
    count, rows, width = key_parts.shape
    slabs = count // SLAB
    vmem = pl.BlockSpec(memory_space=pltpu.VMEM)
    dma = pltpu.SemaphoreType.DMA
    block = (rows, width)
    return pl.pallas_call(
        functools.partial(reduce_kernel, slabs, mp_count),
        out_shape=(
            jax.ShapeDtypeStruct(block, BF),
            jax.ShapeDtypeStruct((count,) + block, BF),
            jax.ShapeDtypeStruct((mp_count,) + block, BF),
        ),
        in_specs=[vmem, vmem],
        out_specs=(vmem, vmem, vmem),
        scratch_shapes=[
            pltpu.VMEM((2, 2, slabs) + block, BF),
            pltpu.VMEM((2, slabs) + block, BF),
            pltpu.VMEM((2, slabs) + block, BF),
            pltpu.VMEM((2, slabs) + block, BF),
            pltpu.VMEM((2, slabs) + block, BF),
            dma((2, 2, slabs)),
            dma((2, slabs)),
            dma((2, slabs)),
            dma((2, 2, slabs)),
            dma((2, slabs)),
            dma((2, slabs)),
            dma((count,)),
            dma((4, count)),
            dma((mp_count,)),
            dma((mp_count,)),
        ],
        compiler_params=pltpu.CompilerParams(
            collective_id=1, has_side_effects=True, vmem_limit_bytes=VMEM_LIMIT
        ),
        cost_estimate=pl.CostEstimate(
            flops=0, bytes_accessed=count * rows * width * 4, transcendentals=0
        ),
        name="reduce_key_value_grads",
    )(key_parts, value_parts)


def dot(a, b):
    return jnp.dot(a, b, preferred_element_type=F32)


def attention_kernel(
    kb, keep, bounds, begin_ref, weight_ref, q_ref, g_ref, k_ref, v_ref,
    dq_ref, dk_ref, dv_ref,
    qs, qt, gs, gt, top, total, dotted, dq_acc, pb, sb, block_top, e_all, p_all,
):
    rows = q_ref.shape[0]
    wide = 2 * rows
    lower, upper, first_row = bounds[0], bounds[1], bounds[2]
    for g in range(GROUP):
        cols = slice(g * HD, (g + 1) * HD)
        span = slice(g * rows, (g + 1) * rows)
        q = q_ref[:, cols]
        grad = (g_ref[:, cols].astype(F32) * weight_ref[...]).astype(BF)
        qs[span, :] = q
        gs[span, :] = grad
        qt[:, span] = q.T
        gt[:, span] = grad.T
    dk_ref[...] = jnp.zeros_like(dk_ref)
    dv_ref[...] = jnp.zeros_like(dv_ref)
    dq_acc[...] = jnp.zeros_like(dq_acc)
    top[...] = jnp.full_like(top, NEGATIVE)
    total[...] = jnp.zeros_like(total)
    dotted[...] = jnp.zeros_like(dotted)
    begin = begin_ref[...]
    row_at = first_row + lax.broadcasted_iota(jnp.int32, (1, rows), 1)

    def visible(j):
        at = j * kb + lax.broadcasted_iota(jnp.int32, (kb, rows), 0)
        seen = (at >= begin) & (at <= row_at)
        return jnp.concatenate([seen, seen], axis=1)

    def terms(j, seen, span):
        at = pl.ds(pl.multiple_of(j * kb, kb), kb)
        scores = dot(k_ref[at, :], qt[:, span]) * (SCALE * LOG2E)
        return jnp.where(seen, scores, NEGATIVE), dot(v_ref[at, :], gt[:, span])

    def first(j, _):
        seen = visible(j)
        for tile in range(GROUP // 2):
            span = slice(tile * wide, (tile + 1) * wide)
            scores, grad_probs = terms(j, seen, span)
            old = top[:, span]
            new = jnp.maximum(old, jnp.max(scores, axis=0, keepdims=True))
            e = jnp.exp2(scores - new)
            factor = jnp.exp2(old - new)
            top[:, span] = new
            total[:, span] = total[:, span] * factor + jnp.sum(e, axis=0, keepdims=True)
            dotted[:, span] = dotted[:, span] * factor + jnp.sum(
                e * grad_probs, axis=0, keepdims=True
            )
            if keep:
                block_top[j, :, span] = new
                e_all[j, :, span] = e
                p_all[j, :, span] = grad_probs
        return 0

    lax.fori_loop(lower, upper, first, 0)
    total[...] = 1.0 / total[...]
    dotted[...] = dotted[...] * total[...]

    def second(j, _):
        at = pl.ds(pl.multiple_of(j * kb, kb), kb)
        if not keep:
            seen = visible(j)
        for tile in range(GROUP // 2):
            span = slice(tile * wide, (tile + 1) * wide)
            if keep:
                ratio = jnp.exp2(block_top[j, :, span] - top[:, span]) * total[:, span]
                probs = e_all[j, :, span] * ratio
                grad_probs = p_all[j, :, span]
            else:
                scores, grad_probs = terms(j, seen, span)
                probs = jnp.exp2(scores - top[:, span]) * total[:, span]
            pb[:, span] = probs.astype(BF)
            sb[:, span] = (probs * (grad_probs - dotted[:, span])).astype(BF)
        low = sb[...]
        dv_ref[at, :] = dot(pb[...], gs[...]).astype(BF)
        dk_ref[at, :] = (dot(low, qs[...]) * SCALE).astype(BF)
        dq_acc[...] += dot(k_ref[at, :].T, low)
        return 0

    lax.fori_loop(lower, upper, second, 0)
    for g in range(GROUP):
        dq_ref[:, g * HD:(g + 1) * HD] = (
            (dq_acc[:, g * rows:(g + 1) * rows] * SCALE).T.astype(BF)
        )


def attention(bounds, begin, weight, queries, grads, keys, values):
    rows = queries.shape[0]
    total_rows, width = keys.shape
    heads = width // HD
    kb = 256
    keep = total_rows <= 4096
    blocks = total_rows // kb
    span = GROUP * rows
    kept = (blocks, kb, span) if keep else (1, 8, 128)
    whole = lambda shape: pl.BlockSpec(shape, lambda c, b: (0, 0))
    column = lambda r, w: pl.BlockSpec((r, w), lambda c, b: (0, c))
    pairs = rows * GROUP * heads * total_rows
    return pl.pallas_call(
        functools.partial(attention_kernel, kb, keep),
        grid_spec=pltpu.PrefetchScalarGridSpec(
            num_scalar_prefetch=1,
            grid=(heads,),
            in_specs=[
                whole((1, rows)),
                whole((rows, 1)),
                column(rows, GROUP * HD),
                column(rows, GROUP * HD),
                column(total_rows, HD),
                column(total_rows, HD),
            ],
            out_specs=[
                column(rows, GROUP * HD),
                column(total_rows, HD),
                column(total_rows, HD),
            ],
            scratch_shapes=[
                pltpu.VMEM((span, HD), BF),
                pltpu.VMEM((HD, span), BF),
                pltpu.VMEM((span, HD), BF),
                pltpu.VMEM((HD, span), BF),
                pltpu.VMEM((1, span), F32),
                pltpu.VMEM((1, span), F32),
                pltpu.VMEM((1, span), F32),
                pltpu.VMEM((HD, span), F32),
                pltpu.VMEM((kb, span), BF),
                pltpu.VMEM((kb, span), BF),
                pltpu.VMEM((blocks, 1, span), F32),
                pltpu.VMEM(kept, F32),
                pltpu.VMEM(kept, F32),
            ],
        ),
        out_shape=(
            jax.ShapeDtypeStruct(queries.shape, BF),
            jax.ShapeDtypeStruct(keys.shape, BF),
            jax.ShapeDtypeStruct(keys.shape, BF),
        ),
        compiler_params=pltpu.CompilerParams(vmem_limit_bytes=VMEM_LIMIT),
        cost_estimate=pl.CostEstimate(
            flops=5 * pairs * HD, bytes_accessed=total_rows * width * 8, transcendentals=pairs
        ),
        name="attention_backward",
    )(bounds, begin, weight, queries, grads, keys, values)


def on_device(
    sublayer_input, rotated_queries, rotated_keys, output_grad, value_weight,
    segment_ids, label_positions,
):
    rows = sublayer_input.shape[0]
    count = lax.axis_size("ctx")
    mp_count = lax.axis_size("mp")
    total_rows = rows * count
    width = rotated_keys.shape[1]
    first_row = lax.axis_index("ctx") * rows
    own = first_row + jnp.arange(rows, dtype=jnp.int32)
    labelled = jnp.any(own[:, None] == label_positions[None, :], axis=1)
    weight = jnp.where(labelled, 4.0, 1.0).astype(F32)[:, None]
    own_segments = lax.dynamic_slice_in_dim(segment_ids, first_row, rows)
    begin = jnp.sum(
        (segment_ids[:, None] < own_segments[None, :]).astype(jnp.int32), axis=0, dtype=jnp.int32
    )
    bounds = jnp.stack([begin[0] // 256, (first_row + rows - 1) // 256 + 1, first_row])
    values = dot(sublayer_input, value_weight).astype(BF)
    input_columns = lax.all_to_all(
        sublayer_input, "ctx", split_axis=1, concat_axis=0, tiled=True
    )
    weight_rows = lax.all_to_all(value_weight, "mp", split_axis=0, concat_axis=1, tiled=True)
    all_keys, all_values = gather_blocks(rotated_keys, values, count)
    query_grad, key_parts, value_parts = attention(
        bounds.astype(jnp.int32), begin[None, :], weight, rotated_queries, output_grad,
        all_keys.reshape(total_rows, width), all_values.reshape(total_rows, width),
    )
    key_grad, all_value_grad, pair_value_grad = reduce_blocks(
        key_parts.reshape(count, rows, width), value_parts.reshape(count, rows, width), mp_count
    )
    joined = jnp.concatenate([pair_value_grad[i] for i in range(mp_count)], axis=1)
    input_grad = lax.dot_general(
        joined, weight_rows, (((1,), (1,)), ((), ())), preferred_element_type=F32
    ).astype(BF)
    value_weight_grad = lax.dot_general(
        input_columns, all_value_grad.reshape(total_rows, width), (((0,), (0,)), ((), ())),
        preferred_element_type=F32,
    ).astype(BF)
    return (query_grad, key_grad, input_grad, value_weight_grad)


def solution(mesh):
    placed = (
        P("ctx", None),
        P("ctx", "mp"),
        P("ctx", "mp"),
        P("ctx", "mp"),
        P(None, "mp"),
        P(),
        P(),
    )
    return jax.shard_map(
        on_device,
        mesh=mesh,
        in_specs=placed,
        out_specs=(P("ctx", "mp"), P("ctx", "mp"), P("ctx", "mp"), P("ctx", "mp")),
        check_vma=False,
    )
```

```python
import functools

import jax
import jax.numpy as jnp
from jax import lax
from jax.experimental import pallas as pl
from jax.experimental.pallas import tpu as pltpu
from jax.sharding import PartitionSpec as P

HEADS = 64
KV_HEADS = 8
HD = 128
GROUP = HEADS // KV_HEADS
SCALE = HD ** (-0.5)
LOG2E = 1.4426950408889634
NEGATIVE = -1e30
MESH = pl.DeviceIdType.MESH
SLAB = 4
CORE = 1
SIDE = 2
BF = jnp.bfloat16
F32 = jnp.float32
VMEM_LIMIT = 56 * 1024 * 1024


def remote(src, dst, send, recv, axis, index):
    return pltpu.make_async_remote_copy(
        src_ref=src,
        dst_ref=dst,
        send_sem=send,
        recv_sem=recv,
        device_id={axis: index},
        device_id_type=MESH,
    )


def flip(pos, bit):
    if bit == CORE:
        return pos + 1 - 2 * lax.rem(pos, 2)
    return lax.rem(pos + 2, SLAB)


def dot(a, b):
    return jnp.dot(a, b, preferred_element_type=F32)


def greet(me, count, mp_count):
    barrier = pltpu.get_barrier_semaphore()

    def along(d, _):
        peer = lax.rem(me + d, count)
        pl.semaphore_signal(barrier, inc=1, device_id={"ctx": peer}, device_id_type=MESH)
        return 0

    lax.fori_loop(1, count, along, 0)
    mine = lax.axis_index("mp")
    for d in range(1, mp_count):
        peer = lax.rem(mine + d, mp_count)
        pl.semaphore_signal(barrier, inc=1, device_id={"mp": peer}, device_id_type=MESH)
    pl.semaphore_wait(barrier, count - 1 + mp_count - 1)


def repeat(low, high, body):
    def step(i, _):
        body(i)
        return 0

    lax.fori_loop(low, high, step, 0)


def kernel(
    count, mp_count, heads, keep, x_split,
    begin_ref, weight_ref, q_ref, g_ref, k_ref, v_ref, x_ref, w_ref,
    dq_ref, dk_ref, ig_ref, wg_ref,
    kv, part, rc, ry, rz, sy, sz, all_v, pair, xc, xt, wr,
    qs, qt, gs, gt, top, total, dotted, dq_acc, pb, sb, block_top, e_all, p_all, ig_acc,
    g_recv, g_send, rc_sem, ry_sem, rz_sem, sc_sem, sy_sem, sz_sem,
    ag_recv, ag_send, mp_recv, mp_send, x_recv, x_send, xf_recv, xf_send,
    w_recv, w_send, w_own,
):
    rows = q_ref.shape[0]
    wide = 2 * rows
    kb = 2 * rows
    slabs = count // SLAB
    me = lax.axis_index("ctx")
    mine = lax.axis_index("mp")
    slab = me // SLAB
    pos = lax.rem(me, SLAB)
    base = me - pos
    core_pos, side_pos = flip(pos, CORE), flip(pos, SIDE)
    both_pos = flip(side_pos, CORE)
    last = slab == slabs - 1
    first_row = me * rows
    blocks = me // 2 + 1
    greet(me, count, mp_count)

    w_rows = w_ref.shape[0] // mp_count

    def weight_copy(peer, slot):
        at = pl.ds(pl.multiple_of(peer * w_rows, w_rows), w_rows)
        return remote(w_ref.at[at, :], wr.at[slot], w_send.at[peer], w_recv.at[slot], "mp", peer)

    def gather_copy(c, dest, block):
        target = (me + SLAB, base + side_pos, base + core_pos)[dest]
        ref = kv.at[c, block]
        return remote(ref, ref, g_send.at[c, dest, block], g_recv.at[c, block], "ctx", target)

    def gather_own(c):
        cols = pl.ds(pl.multiple_of(c * HD, HD), HD)
        kv[c, me, :, :HD] = k_ref[:, cols]
        kv[c, me, :, HD:] = v_ref[:, cols]

        @pl.when(slab < slabs - 1)
        def _():
            gather_copy(c, 0, me).start()

        gather_copy(c, 1, me).start()
        gather_copy(c, 2, me).start()

    def gather_forward(c):
        def one(k):
            block = (slab - k) * SLAB + pos
            gather_copy(c, 0, block).wait_recv()

            @pl.when(slab < slabs - 1)
            def _():
                gather_copy(c, 0, block).start()

            gather_copy(c, 1, block).start()
            gather_copy(c, 2, block).start()

        repeat(1, slab + 1, one)

    def gather_cross(c):
        def one(k):
            block = (slab - k) * SLAB + side_pos
            gather_copy(c, 1, block).wait_recv()
            gather_copy(c, 2, block).start()

        repeat(0, slab + 1, one)

    def gather_arrive(c):
        def one(s):
            gather_copy(c, 2, s * SLAB + core_pos).wait_recv()
            gather_copy(c, 2, s * SLAB + both_pos).wait_recv()

        repeat(0, slab + 1, one)

    def gather_finish(c):
        def one(s):
            @pl.when(slab < slabs - 1)
            def _():
                gather_copy(c, 0, s * SLAB + pos).wait_send()

            gather_copy(c, 1, s * SLAB + pos).wait_send()
            gather_copy(c, 2, s * SLAB + pos).wait_send()
            gather_copy(c, 2, s * SLAB + side_pos).wait_send()

        repeat(0, slab + 1, one)

    def core_copy(c, which, s):
        block = s * SLAB + (core_pos, both_pos)[which]
        return remote(
            part.at[c, block], rc.at[c, which, s],
            sc_sem.at[c, which, s], rc_sem.at[c, which, s], "ctx", base + core_pos,
        )

    def side_copy(c, s):
        return remote(
            sy.at[c, s], ry.at[c, s], sy_sem.at[c, s], ry_sem.at[c, s], "ctx", base + side_pos
        )

    def down_copy(c, s):
        return remote(
            sz.at[c, s], rz.at[c, s], sz_sem.at[c, s], rz_sem.at[c, s], "ctx", me - SLAB
        )

    def reduce_core(c):
        def one(s):
            core_copy(c, 1, s).start()
            core_copy(c, 0, s).start()

        repeat(0, slab + 1, one)

    def reduce_side(c):
        def one(s):
            core_copy(c, 1, s).wait_recv()
            both = part[c, s * SLAB + side_pos].astype(F32) + rc[c, 1, s].astype(F32)
            sy[c, s] = both.astype(BF)
            side_copy(c, s).start()

        repeat(0, slab + 1, one)

    def slab_total(c, s):
        core_copy(c, 0, s).wait_recv()
        both = part[c, s * SLAB + pos].astype(F32) + rc[c, 0, s].astype(F32)
        side_copy(c, s).wait_recv()
        return both + ry[c, s].astype(F32)

    def reduce_down(c):
        def deliver(s, full):
            @pl.when(s < slab)
            def _():
                sz[c, s] = full.astype(BF)
                down_copy(c, s).start()

            @pl.when(s == slab)
            def _():
                low = full.astype(BF)
                dk_ref[:, pl.ds(pl.multiple_of(c * HD, HD), HD)] = low[:, :HD]
                all_v[c, me] = low[:, HD:]
                pair[mine, c] = low[:, HD:]

        def one(s):
            full = slab_total(c, s)

            @pl.when(slab < slabs - 1)
            def _():
                down_copy(c, s).wait_recv()
                deliver(s, full + rz[c, s].astype(F32))

            @pl.when(last)
            def _():
                deliver(s, full)

        repeat(0, slab + 1, one)
        for d in range(1, mp_count):
            peer = lax.rem(mine + d, mp_count)
            pair_copy(c, peer, mine).start()

        @pl.when(slab < slabs - 1)
        def _():
            spread_copy(c, 0, me).start()

        @pl.when(slab > 0)
        def _():
            spread_copy(c, 1, me).start()

        spread_copy(c, 2, me).start()
        spread_copy(c, 3, me).start()

    def reduce_finish(c):
        def one(s):
            core_copy(c, 0, s).wait_send()
            core_copy(c, 1, s).wait_send()
            side_copy(c, s).wait_send()

            @pl.when(s < slab)
            def _():
                down_copy(c, s).wait_send()

        repeat(0, slab + 1, one)

    def pair_copy(c, peer, slot):
        return remote(
            all_v.at[c, me], pair.at[slot, c], mp_send.at[c, peer], mp_recv.at[c, slot],
            "mp", peer,
        )

    def spread_copy(c, dest, block):
        target = (me + SLAB, me - SLAB, base + side_pos, base + core_pos)[dest]
        ref = all_v.at[c, block]
        return remote(ref, ref, ag_send.at[c, dest, block], ag_recv.at[c, block], "ctx", target)

    def spread_forward(c):
        def one(k):
            low, high = slab - k, slab + k

            @pl.when(high < slabs)
            def _():
                block = high * SLAB + pos
                spread_copy(c, 0, block).wait_recv()

                @pl.when(slab > 0)
                def _():
                    spread_copy(c, 1, block).start()

                spread_copy(c, 2, block).start()
                spread_copy(c, 3, block).start()

            @pl.when(low >= 0)
            def _():
                block = low * SLAB + pos
                spread_copy(c, 0, block).wait_recv()

                @pl.when(slab < slabs - 1)
                def _():
                    spread_copy(c, 0, block).start()

                spread_copy(c, 2, block).start()
                spread_copy(c, 3, block).start()

        repeat(1, slabs, one)

    def spread_cross(c):
        def one(s):
            block = s * SLAB + side_pos
            spread_copy(c, 2, block).wait_recv()
            spread_copy(c, 3, block).start()

        repeat(0, slabs, one)

    def spread_arrive(c):
        def one(s):
            spread_copy(c, 3, s * SLAB + core_pos).wait_recv()
            spread_copy(c, 3, s * SLAB + both_pos).wait_recv()

        repeat(0, slabs, one)

    def spread_finish(c):
        def one(s):
            own = s * SLAB + pos

            @pl.when((s <= slab) & (slab < slabs - 1))
            def _():
                spread_copy(c, 0, own).wait_send()

            @pl.when((s >= slab) & (slab > 0))
            def _():
                spread_copy(c, 1, own).wait_send()

            spread_copy(c, 2, own).wait_send()
            spread_copy(c, 3, own).wait_send()
            spread_copy(c, 3, s * SLAB + side_pos).wait_send()

        repeat(0, slabs, one)

    owner = lax.rem(me, mp_count) == mine
    x_cols = xc.shape[2]

    def x_piece(t):
        if x_split:
            return x_ref.at[t]
        return x_ref.at[:, pl.ds(pl.multiple_of(t * x_cols, x_cols), x_cols)]

    def x_copy(t, slot):
        return remote(x_piece(t), xc.at[slot], x_send.at[t], x_recv.at[slot], "ctx", t)

    def x_start():
        @pl.when(owner)
        def _():
            xc[me] = x_piece(me)[...]

        def one(i):
            t = lax.rem(i * mp_count + mine + (me // mp_count) * mp_count, count)

            @pl.when(t != me)
            def _():
                x_copy(t, me).start()

        repeat(0, count // mp_count, one)

    def x_over(peer):
        return remote(xc, xc, xf_send.at[peer], xf_recv, "mp", peer)

    def x_forward():
        @pl.when(owner)
        def _():
            def one(d):
                peer = lax.rem(me + d, count)
                x_copy(peer, peer).wait_recv()

            repeat(1, count, one)
            for d in range(1, mp_count):
                x_over(lax.rem(mine + d, mp_count)).start()

    def x_arrive():
        if mp_count > 1:
            @pl.when(jnp.logical_not(owner))
            def _():
                x_over(lax.rem(mine + 1, mp_count)).wait_recv()

    def x_finish():
        def one(i):
            t = i * mp_count + mine

            @pl.when(t != me)
            def _():
                x_copy(t, me).wait_send()

        repeat(0, count // mp_count, one)

        @pl.when(owner)
        def _():
            for d in range(1, mp_count):
                x_over(lax.rem(mine + d, mp_count)).wait_send()

    begin = begin_ref[...]
    row_at = first_row + lax.broadcasted_iota(jnp.int32, (1, rows), 1)

    def visible(j):
        at = j * kb + lax.broadcasted_iota(jnp.int32, (kb, rows), 0)
        seen = (at >= begin) & (at <= row_at)
        return jnp.concatenate([seen, seen], axis=1)

    def key_block(c, j):
        return kv[c, pl.ds(2 * j, 2), :, :HD].reshape(kb, HD)

    def value_block(c, j):
        return kv[c, pl.ds(2 * j, 2), :, HD:].reshape(kb, HD)

    def terms(c, j, seen, span):
        scores = dot(key_block(c, j), qt[:, span]) * (SCALE * LOG2E)
        return jnp.where(seen, scores, NEGATIVE), dot(value_block(c, j), gt[:, span])

    def prepare(c):
        for g in range(GROUP):
            cols = pl.ds(pl.multiple_of((c * GROUP + g) * HD, HD), HD)
            span = slice(g * rows, (g + 1) * rows)
            q = q_ref[:, cols]
            grad = (g_ref[:, cols].astype(F32) * weight_ref[...]).astype(BF)
            qs[span, :] = q
            gs[span, :] = grad
            qt[:, span] = q.T
            gt[:, span] = grad.T
        dq_acc[...] = jnp.zeros_like(dq_acc)
        top[...] = jnp.full_like(top, NEGATIVE)
        total[...] = jnp.zeros_like(total)
        dotted[...] = jnp.zeros_like(dotted)

    def first_pass(c):
        def one(j):
            seen = visible(j)
            for tile in range(GROUP // 2):
                span = slice(tile * wide, (tile + 1) * wide)
                scores, grad_probs = terms(c, j, seen, span)
                old = top[:, span]
                new = jnp.maximum(old, jnp.max(scores, axis=0, keepdims=True))
                e = jnp.exp2(scores - new)
                factor = jnp.exp2(old - new)
                top[:, span] = new
                total[:, span] = total[:, span] * factor + jnp.sum(e, axis=0, keepdims=True)
                dotted[:, span] = dotted[:, span] * factor + jnp.sum(
                    e * grad_probs, axis=0, keepdims=True
                )
                if keep:
                    block_top[j, :, span] = new
                    e_all[j, :, span] = e
                    p_all[j, :, span] = grad_probs

        repeat(0, blocks, one)
        total[...] = 1.0 / total[...]
        dotted[...] = dotted[...] * total[...]

    def second_pass(c):
        for i in range(SLAB):
            part[c, base + i] = jnp.zeros((rows, 2 * HD), BF)

        def one(j):
            if not keep:
                seen = visible(j)
            for tile in range(GROUP // 2):
                span = slice(tile * wide, (tile + 1) * wide)
                if keep:
                    ratio = jnp.exp2(block_top[j, :, span] - top[:, span]) * total[:, span]
                    probs = e_all[j, :, span] * ratio
                    grad_probs = p_all[j, :, span]
                else:
                    scores, grad_probs = terms(c, j, seen, span)
                    probs = jnp.exp2(scores - top[:, span]) * total[:, span]
                pb[:, span] = probs.astype(BF)
                sb[:, span] = (probs * (grad_probs - dotted[:, span])).astype(BF)
            low = sb[...]
            at = pl.ds(2 * j, 2)
            value_term = dot(pb[...], gs[...]).astype(BF)
            key_term = (dot(low, qs[...]) * SCALE).astype(BF)
            part[c, at, :, HD:] = value_term.reshape(2, rows, HD)
            part[c, at, :, :HD] = key_term.reshape(2, rows, HD)
            dq_acc[...] += dot(key_block(c, j).T, low)

        repeat(0, blocks, one)
        for g in range(GROUP):
            cols = pl.ds(pl.multiple_of((c * GROUP + g) * HD, HD), HD)
            dq_ref[:, cols] = (dq_acc[:, g * rows:(g + 1) * rows] * SCALE).T.astype(BF)

    repeat(0, heads, gather_own)
    for d in range(1, mp_count):
        weight_copy(lax.rem(mine + d, mp_count), mine).start()
    own_rows = pl.ds(pl.multiple_of(mine * w_rows, w_rows), w_rows)
    own_weight = pltpu.make_async_copy(w_ref.at[own_rows, :], wr.at[mine], w_own)
    own_weight.start()
    early = slab < slabs // 2
    ahead = jnp.where(early, heads, 1)

    def gather_both(c):
        gather_forward(c)
        gather_cross(c)

    repeat(0, ahead, gather_both)

    def head(c):
        prepare(c)
        gather_arrive(c)

        @pl.when(c == min(1, heads - 1))
        def _():
            x_start()

        first_pass(c)

        @pl.when((c < heads - 1) & jnp.logical_not(early))
        def _():
            gather_forward(c + 1)

        @pl.when(c > 0)
        def _():
            reduce_side(c - 1)

        second_pass(c)
        reduce_core(c)

        @pl.when((c < heads - 1) & jnp.logical_not(early))
        def _():
            gather_cross(c + 1)

        @pl.when(c > 0)
        def _():
            reduce_down(c - 1)

        @pl.when(c > 1)
        def _():
            spread_forward(c - 2)

    repeat(0, heads, head)
    final = heads - 1
    reduce_side(final)
    x_forward()
    reduce_down(final)
    if heads > 1:
        spread_forward(heads - 2)
    spread_forward(final)

    repeat(0, heads, spread_cross)
    x_arrive()
    for i in range(count):
        xt[:, i * rows:(i + 1) * rows] = xc[i].T
    own_weight.wait()
    for d in range(1, mp_count):
        peer = lax.rem(mine + d, mp_count)
        weight_copy(peer, peer).wait_recv()
        for c in range(heads):
            pair_copy(c, peer, peer).wait_recv()

    contract = (((1,), (1,)), ((), ()))

    def input_term(m):
        for c in range(heads):
            term = lax.dot_general(
                pair[m, c], wr[m, :, c * HD:(c + 1) * HD], contract,
                preferred_element_type=F32,
            )
            ig_acc[...] += term

    ig_acc[...] = jnp.zeros_like(ig_acc)
    repeat(0, mp_count, input_term)
    ig_ref[...] = ig_acc[...].astype(BF)
    for c in range(heads):
        spread_arrive(c)
        wg_ref[:, c * HD:(c + 1) * HD] = dot(
            xt[...], all_v[c].reshape(count * rows, HD)
        ).astype(BF)

    for d in range(1, mp_count):
        peer = lax.rem(mine + d, mp_count)
        weight_copy(peer, mine).wait_send()
        for c in range(heads):
            pair_copy(c, peer, mine).wait_send()
    x_finish()
    repeat(0, heads, gather_finish)
    repeat(0, heads, reduce_finish)
    repeat(0, heads, spread_finish)


def on_device(
    sublayer_input, rotated_queries, rotated_keys, output_grad, value_weight,
    segment_ids, label_positions,
):
    rows, features = sublayer_input.shape
    count = lax.axis_size("ctx")
    mp_count = lax.axis_size("mp")
    slabs = count // SLAB
    total_rows = rows * count
    width = rotated_keys.shape[1]
    heads = width // HD
    span = GROUP * rows
    kb = 2 * rows
    first_row = lax.axis_index("ctx") * rows
    own = first_row + jnp.arange(rows, dtype=jnp.int32)
    labelled = jnp.any(own[:, None] == label_positions[None, :], axis=1)
    weight = jnp.where(labelled, 4.0, 1.0).astype(F32)[:, None]
    own_segments = lax.dynamic_slice_in_dim(segment_ids, first_row, rows)
    begin = jnp.sum(
        (segment_ids[:, None] < own_segments[None, :]).astype(jnp.int32), axis=0, dtype=jnp.int32
    )
    values = dot(sublayer_input, value_weight).astype(BF)
    x_cols = features // count
    x_split = x_cols % 128 != 0
    pieces = sublayer_input
    if x_split:
        pieces = sublayer_input.reshape(rows, count, x_cols).transpose(1, 0, 2)
    keep = total_rows <= 4096
    kept = (total_rows // kb, kb, span) if keep else (1, 8, 128)
    vmem = pl.BlockSpec(memory_space=pltpu.VMEM)
    anywhere = pl.BlockSpec(memory_space=pl.ANY)
    dma = pltpu.SemaphoreType.DMA
    chunk = (rows, 2 * HD)
    pairs = rows * GROUP * heads * total_rows
    return pl.pallas_call(
        functools.partial(kernel, count, mp_count, heads, keep, x_split),
        out_shape=(
            jax.ShapeDtypeStruct(rotated_queries.shape, BF),
            jax.ShapeDtypeStruct((rows, width), BF),
            jax.ShapeDtypeStruct((rows, features // mp_count), BF),
            jax.ShapeDtypeStruct((x_cols, width), BF),
        ),
        in_specs=[vmem] * 7 + [anywhere],
        out_specs=(vmem,) * 4,
        scratch_shapes=[
            pltpu.VMEM((heads, count) + chunk, BF),
            pltpu.VMEM((heads, count) + chunk, BF),
            pltpu.VMEM((heads, 2, slabs) + chunk, BF),
            pltpu.VMEM((heads, slabs) + chunk, BF),
            pltpu.VMEM((heads, slabs) + chunk, BF),
            pltpu.VMEM((heads, slabs) + chunk, BF),
            pltpu.VMEM((heads, slabs) + chunk, BF),
            pltpu.VMEM((heads, count, rows, HD), BF),
            pltpu.VMEM((mp_count, heads, rows, HD), BF),
            pltpu.VMEM((count, rows, x_cols), BF),
            pltpu.VMEM((x_cols, total_rows), BF),
            pltpu.VMEM((mp_count, features // mp_count, width), BF),
            pltpu.VMEM((span, HD), BF),
            pltpu.VMEM((HD, span), BF),
            pltpu.VMEM((span, HD), BF),
            pltpu.VMEM((HD, span), BF),
            pltpu.VMEM((1, span), F32),
            pltpu.VMEM((1, span), F32),
            pltpu.VMEM((1, span), F32),
            pltpu.VMEM((HD, span), F32),
            pltpu.VMEM((kb, span), BF),
            pltpu.VMEM((kb, span), BF),
            pltpu.VMEM((total_rows // kb, 1, span), F32),
            pltpu.VMEM(kept, F32),
            pltpu.VMEM(kept, F32),
            pltpu.VMEM((rows, features // mp_count), F32),
            dma((heads, count)),
            dma((heads, 3, count)),
            dma((heads, 2, slabs)),
            dma((heads, slabs)),
            dma((heads, slabs)),
            dma((heads, 2, slabs)),
            dma((heads, slabs)),
            dma((heads, slabs)),
            dma((heads, count)),
            dma((heads, 4, count)),
            dma((heads, mp_count)),
            dma((heads, mp_count)),
            dma((count,)),
            dma((count,)),
            dma,
            dma((mp_count,)),
            dma((mp_count,)),
            dma((mp_count,)),
            dma,
        ],
        compiler_params=pltpu.CompilerParams(
            collective_id=0, has_side_effects=True, vmem_limit_bytes=VMEM_LIMIT
        ),
        cost_estimate=pl.CostEstimate(
            flops=5 * pairs * HD, bytes_accessed=total_rows * width * 8, transcendentals=pairs
        ),
        name="attention_backward",
    )(begin[None, :], weight, rotated_queries, output_grad, rotated_keys, values, pieces,
      value_weight)


def solution(mesh):
    placed = (
        P("ctx", None),
        P("ctx", "mp"),
        P("ctx", "mp"),
        P("ctx", "mp"),
        P(None, "mp"),
        P(),
        P(),
    )
    return jax.shard_map(
        on_device,
        mesh=mesh,
        in_specs=placed,
        out_specs=(P("ctx", "mp"), P("ctx", "mp"), P("ctx", "mp"), P("ctx", "mp")),
        check_vma=False,
    )
```

```python
import functools

import jax
import jax.numpy as jnp
from jax import lax
from jax.experimental import pallas as pl
from jax.experimental.pallas import tpu as pltpu
from jax.sharding import PartitionSpec as P

HEADS = 64
KV_HEADS = 8
HD = 128
GROUP = HEADS // KV_HEADS
SCALE = HD ** (-0.5)
LOG2E = 1.4426950408889634
NEGATIVE = -1e30
MESH = pl.DeviceIdType.MESH
SLAB = 4
CORE = 1
SIDE = 2
BF = jnp.bfloat16
F32 = jnp.float32
VMEM_LIMIT = 56 * 1024 * 1024


def remote(src, dst, send, recv, axis, index):
    return pltpu.make_async_remote_copy(
        src_ref=src,
        dst_ref=dst,
        send_sem=send,
        recv_sem=recv,
        device_id={axis: index},
        device_id_type=MESH,
    )


def flip(pos, bit):
    if bit == CORE:
        return pos + 1 - 2 * lax.rem(pos, 2)
    return lax.rem(pos + 2, SLAB)


def dot(a, b):
    return jnp.dot(a, b, preferred_element_type=F32)


def greet(me, count, mp_count):
    barrier = pltpu.get_barrier_semaphore()

    def along(d, _):
        peer = lax.rem(me + d, count)
        pl.semaphore_signal(barrier, inc=1, device_id={"ctx": peer}, device_id_type=MESH)
        return 0

    lax.fori_loop(1, count, along, 0)
    mine = lax.axis_index("mp")
    for d in range(1, mp_count):
        peer = lax.rem(mine + d, mp_count)
        pl.semaphore_signal(barrier, inc=1, device_id={"mp": peer}, device_id_type=MESH)
    return barrier


def repeat(low, high, body):
    def step(i, _):
        body(i)
        return 0

    lax.fori_loop(low, high, step, 0)


def kernel(
    count, mp_count, heads, keep, x_split,
    seg_ref, label_ref, q_ref, g_ref, k_ref, x_ref, w_ref,
    dq_ref, dk_ref, ig_ref, wg_ref,
    kv, part, rc, ry, rz, sy, sz, all_v, pair, xc, xt, wr,
    qs, qt, gs, gt, top, total, dotted, dq_acc, pb, sb, block_top, e_all, p_all, ig_acc,
    g_recv, g_send, gz_send, rc_sem, ry_sem, rz_sem, sc_sem, sy_sem, sz_sem,
    ag_recv, ag_send, agz_send, mp_recv, mp_send, x_recv, x_send, xf_recv, xf_send,
    w_recv, w_send,
):
    rows = q_ref.shape[0]
    wide = 2 * rows
    kb = 2 * rows
    slabs = count // SLAB
    me = lax.axis_index("ctx")
    mine = lax.axis_index("mp")
    slab = me // SLAB
    pos = lax.rem(me, SLAB)
    base = me - pos
    core_pos, side_pos = flip(pos, CORE), flip(pos, SIDE)
    both_pos = flip(side_pos, CORE)
    first_row = me * rows
    blocks = me // 2 + 1
    barrier = greet(me, count, mp_count)

    if x_split:
        values = jnp.zeros((rows, k_ref.shape[1]), F32)
        for t in range(count):
            values += dot(x_ref[t], w_ref[t * xc.shape[2]:(t + 1) * xc.shape[2], :])
    else:
        values = dot(x_ref[...], w_ref[...])
    values = values.astype(BF)
    position = first_row + lax.broadcasted_iota(jnp.int32, (rows, label_ref.shape[1]), 0)
    loss_weight = jnp.max(
        jnp.where(position == label_ref[...], 4.0, 1.0).astype(F32), axis=1, keepdims=True
    )
    segments = seg_ref[...]
    own_segments = seg_ref[:, pl.ds(pl.multiple_of(first_row, rows), rows)]
    begin = jnp.zeros((1, rows), jnp.int32)
    for v in range(1, 4):
        before = jnp.sum(jnp.where(segments < v, 1.0, 0.0), axis=1, keepdims=True)
        begin = jnp.where(own_segments == v, before.astype(jnp.int32), begin)
    pl.semaphore_wait(barrier, count - 1 + mp_count - 1)

    w_rows = w_ref.shape[0] // mp_count

    def weight_copy(peer, slot):
        at = pl.ds(pl.multiple_of(peer * w_rows, w_rows), w_rows)
        return remote(w_ref.at[at, :], wr.at[slot], w_send.at[peer], w_recv.at[slot], "mp", peer)

    def gather_copy(c, dest, block):
        target = (base + side_pos, base + core_pos)[dest]
        ref = kv.at[c, block]
        return remote(ref, ref, g_send.at[c, dest, block], g_recv.at[c, block], "ctx", target)

    def gather_up(c, t):
        ref = kv.at[c, me]
        return remote(ref, ref, gz_send.at[c, t], g_recv.at[c, me], "ctx", t * SLAB + pos)

    def gather_own(c):
        cols = pl.ds(pl.multiple_of(c * HD, HD), HD)
        kv[c, me, :, :HD] = k_ref[:, cols]
        repeat(slab + 1, slabs, lambda t: gather_up(c, t).start())
        gather_copy(c, 0, me).start()
        gather_copy(c, 1, me).start()

    def gather_forward(c):
        def one(k):
            block = (slab - k) * SLAB + pos
            gather_copy(c, 0, block).wait_recv()
            gather_copy(c, 0, block).start()
            gather_copy(c, 1, block).start()

        repeat(1, slab + 1, one)

    def gather_cross(c):
        def one(k):
            block = (slab - k) * SLAB + side_pos
            gather_copy(c, 0, block).wait_recv()
            gather_copy(c, 1, block).start()

        repeat(0, slab + 1, one)

    def gather_arrive(c):
        def one(s):
            gather_copy(c, 1, s * SLAB + core_pos).wait_recv()
            gather_copy(c, 1, s * SLAB + both_pos).wait_recv()

        repeat(0, slab + 1, one)

    def gather_finish(c):
        def one(s):
            gather_copy(c, 0, s * SLAB + pos).wait_send()
            gather_copy(c, 1, s * SLAB + pos).wait_send()
            gather_copy(c, 1, s * SLAB + side_pos).wait_send()

        repeat(0, slab + 1, one)
        repeat(slab + 1, slabs, lambda t: gather_up(c, t).wait_send())

    def core_copy(c, which, s):
        block = s * SLAB + (core_pos, both_pos)[which]
        return remote(
            part.at[c, block], rc.at[c, which, s],
            sc_sem.at[c, which, s], rc_sem.at[c, which, s], "ctx", base + core_pos,
        )

    def side_copy(c, s):
        return remote(
            sy.at[c, s], ry.at[c, s], sy_sem.at[c, s], ry_sem.at[c, s], "ctx", base + side_pos
        )

    def down_copy(c, s):
        return remote(
            sz.at[c, s], rz.at[c, slab], sz_sem.at[c, s], rz_sem.at[c, slab],
            "ctx", s * SLAB + pos,
        )

    def down_arrival(c, t):
        return remote(
            sz.at[c, t], rz.at[c, t], sz_sem.at[c, t], rz_sem.at[c, t], "ctx", base + core_pos
        )

    def reduce_core(c):
        def one(s):
            core_copy(c, 1, s).start()
            core_copy(c, 0, s).start()

        repeat(0, slab + 1, one)

    def reduce_side(c):
        def one(s):
            core_copy(c, 1, s).wait_recv()
            both = part[c, s * SLAB + side_pos].astype(F32) + rc[c, 1, s].astype(F32)
            sy[c, s] = both.astype(BF)
            side_copy(c, s).start()

        repeat(0, slab + 1, one)

    def slab_total(c, s):
        core_copy(c, 0, s).wait_recv()
        both = part[c, s * SLAB + pos].astype(F32) + rc[c, 0, s].astype(F32)
        side_copy(c, s).wait_recv()
        return both + ry[c, s].astype(F32)

    def reduce_send(c):
        def one(s):
            sz[c, s] = slab_total(c, s).astype(BF)
            down_copy(c, s).start()

        repeat(0, slab, one)

    def reduce_final(c):
        def one(t, full):
            down_arrival(c, t).wait_recv()
            return full + rz[c, t].astype(F32)

        low = lax.fori_loop(slab + 1, slabs, one, slab_total(c, slab)).astype(BF)
        dk_ref[:, pl.ds(pl.multiple_of(c * HD, HD), HD)] = low[:, :HD]
        all_v[c, me] = low[:, HD:]
        pair[mine, c] = low[:, HD:]
        repeat(1, slabs, lambda k: spread_far(c, k).start())
        spread_copy(c, 0, me).start()
        spread_copy(c, 1, me).start()
        for d in range(1, mp_count):
            pair_copy(c, lax.rem(mine + d, mp_count), mine).start()

    def reduce_finish(c):
        def one(s):
            core_copy(c, 0, s).wait_send()
            core_copy(c, 1, s).wait_send()
            side_copy(c, s).wait_send()

            @pl.when(s < slab)
            def _():
                down_copy(c, s).wait_send()

        repeat(0, slab + 1, one)

    def pair_copy(c, peer, slot):
        return remote(
            all_v.at[c, me], pair.at[slot, c], mp_send.at[c, peer], mp_recv.at[c, slot],
            "mp", peer,
        )

    def spread_copy(c, dest, block):
        target = (base + side_pos, base + core_pos)[dest]
        ref = all_v.at[c, block]
        return remote(ref, ref, ag_send.at[c, dest, block], ag_recv.at[c, block], "ctx", target)

    def spread_far(c, k):
        t = lax.rem(slab + k, slabs)
        ref = all_v.at[c, me]
        return remote(ref, ref, agz_send.at[c, t], ag_recv.at[c, me], "ctx", t * SLAB + pos)

    def spread_forward(c):
        def one(k):
            block = lax.rem(slab + k, slabs) * SLAB + pos
            spread_copy(c, 0, block).wait_recv()
            spread_copy(c, 0, block).start()
            spread_copy(c, 1, block).start()

        repeat(1, slabs, one)

    def spread_cross(c):
        def one(k):
            block = lax.rem(slab + k, slabs) * SLAB + side_pos
            spread_copy(c, 0, block).wait_recv()
            spread_copy(c, 1, block).start()

        repeat(0, slabs, one)

    def spread_arrive(c):
        def one(s):
            spread_copy(c, 1, s * SLAB + core_pos).wait_recv()
            spread_copy(c, 1, s * SLAB + both_pos).wait_recv()

        repeat(0, slabs, one)

    def spread_finish(c):
        def one(s):
            spread_copy(c, 0, s * SLAB + pos).wait_send()
            spread_copy(c, 1, s * SLAB + pos).wait_send()
            spread_copy(c, 1, s * SLAB + side_pos).wait_send()

        repeat(0, slabs, one)
        repeat(1, slabs, lambda k: spread_far(c, k).wait_send())

    owner = lax.rem(me, mp_count) == mine
    x_cols = xc.shape[2]

    def x_piece(t):
        if x_split:
            return x_ref.at[t]
        return x_ref.at[:, pl.ds(pl.multiple_of(t * x_cols, x_cols), x_cols)]

    def x_copy(t, slot):
        return remote(x_piece(t), xc.at[slot], x_send.at[t], x_recv.at[slot], "ctx", t)

    def x_start():
        @pl.when(owner)
        def _():
            xc[me] = x_piece(me)[...]

        def one(i):
            t = lax.rem(i * mp_count + mine + (me // mp_count) * mp_count, count)

            @pl.when(t != me)
            def _():
                x_copy(t, me).start()

        repeat(0, count // mp_count, one)

    def x_over(peer):
        return remote(xc, xc, xf_send.at[peer], xf_recv, "mp", peer)

    def x_forward():
        @pl.when(owner)
        def _():
            def one(d):
                peer = lax.rem(me + d, count)
                x_copy(peer, peer).wait_recv()

            repeat(1, count, one)
            for d in range(1, mp_count):
                x_over(lax.rem(mine + d, mp_count)).start()

    def x_arrive():
        if mp_count > 1:
            @pl.when(jnp.logical_not(owner))
            def _():
                x_over(lax.rem(mine + 1, mp_count)).wait_recv()

    def x_finish():
        def one(i):
            t = i * mp_count + mine

            @pl.when(t != me)
            def _():
                x_copy(t, me).wait_send()

        repeat(0, count // mp_count, one)

        @pl.when(owner)
        def _():
            for d in range(1, mp_count):
                x_over(lax.rem(mine + d, mp_count)).wait_send()

    row_at = first_row + lax.broadcasted_iota(jnp.int32, (1, rows), 1)

    def visible(j):
        at = j * kb + lax.broadcasted_iota(jnp.int32, (kb, rows), 0)
        seen = (at >= begin) & (at <= row_at)
        return jnp.concatenate([seen, seen], axis=1)

    def key_block(c, j):
        return kv[c, pl.ds(2 * j, 2), :, :HD].reshape(kb, HD)

    def value_block(c, j):
        return kv[c, pl.ds(2 * j, 2), :, HD:].reshape(kb, HD)

    def terms(c, j, seen, span):
        scores = dot(key_block(c, j), qt[:, span]) * (SCALE * LOG2E)
        return jnp.where(seen, scores, NEGATIVE), dot(value_block(c, j), gt[:, span])

    def prepare(c):
        for g in range(GROUP):
            cols = pl.ds(pl.multiple_of((c * GROUP + g) * HD, HD), HD)
            span = slice(g * rows, (g + 1) * rows)
            q = q_ref[:, cols]
            grad = (g_ref[:, cols].astype(F32) * loss_weight).astype(BF)
            qs[span, :] = q
            gs[span, :] = grad
            qt[:, span] = q.T
            gt[:, span] = grad.T
        dq_acc[...] = jnp.zeros_like(dq_acc)
        top[...] = jnp.full_like(top, NEGATIVE)
        total[...] = jnp.zeros_like(total)
        dotted[...] = jnp.zeros_like(dotted)

    def first_pass(c):
        def one(j):
            seen = visible(j)
            for tile in range(GROUP // 2):
                span = slice(tile * wide, (tile + 1) * wide)
                scores, grad_probs = terms(c, j, seen, span)
                old = top[:, span]
                new = jnp.maximum(old, jnp.max(scores, axis=0, keepdims=True))
                e = jnp.exp2(scores - new)
                factor = jnp.exp2(old - new)
                top[:, span] = new
                total[:, span] = total[:, span] * factor + jnp.sum(e, axis=0, keepdims=True)
                dotted[:, span] = dotted[:, span] * factor + jnp.sum(
                    e * grad_probs, axis=0, keepdims=True
                )
                if keep:
                    block_top[j, :, span] = new
                    e_all[j, :, span] = e
                    p_all[j, :, span] = grad_probs

        repeat(0, blocks, one)
        total[...] = 1.0 / total[...]
        dotted[...] = dotted[...] * total[...]

    def second_pass(c):
        for i in range(SLAB):
            part[c, base + i] = jnp.zeros((rows, 2 * HD), BF)

        def one(j):
            if not keep:
                seen = visible(j)
            for tile in range(GROUP // 2):
                span = slice(tile * wide, (tile + 1) * wide)
                if keep:
                    ratio = jnp.exp2(block_top[j, :, span] - top[:, span]) * total[:, span]
                    probs = e_all[j, :, span] * ratio
                    grad_probs = p_all[j, :, span]
                else:
                    scores, grad_probs = terms(c, j, seen, span)
                    probs = jnp.exp2(scores - top[:, span]) * total[:, span]
                pb[:, span] = probs.astype(BF)
                sb[:, span] = (probs * (grad_probs - dotted[:, span])).astype(BF)
            low = sb[...]
            at = pl.ds(2 * j, 2)
            value_term = dot(pb[...], gs[...]).astype(BF)
            key_term = (dot(low, qs[...]) * SCALE).astype(BF)
            part[c, at, :, HD:] = value_term.reshape(2, rows, HD)
            part[c, at, :, :HD] = key_term.reshape(2, rows, HD)
            dq_acc[...] += dot(key_block(c, j).T, low)

        repeat(0, blocks, one)
        for g in range(GROUP):
            cols = pl.ds(pl.multiple_of((c * GROUP + g) * HD, HD), HD)
            dq_ref[:, cols] = (dq_acc[:, g * rows:(g + 1) * rows] * SCALE).T.astype(BF)

    for c in range(heads):
        kv[c, me, :, HD:] = values[:, c * HD:(c + 1) * HD]
    repeat(0, heads, gather_own)
    for d in range(1, mp_count):
        weight_copy(lax.rem(mine + d, mp_count), mine).start()

    early = slab < slabs // 2
    ahead = jnp.where(early, heads, 1)

    def gather_both(c):
        gather_forward(c)
        gather_cross(c)

    repeat(0, ahead, gather_both)

    def head(c):
        prepare(c)
        gather_arrive(c)

        @pl.when(c == min(1, heads - 1))
        def _():
            x_start()

        first_pass(c)

        @pl.when((c < heads - 1) & jnp.logical_not(early))
        def _():
            gather_forward(c + 1)

        @pl.when(c > 0)
        def _():
            reduce_side(c - 1)

        @pl.when(c > 1)
        def _():
            reduce_final(c - 2)

        second_pass(c)
        reduce_core(c)

        @pl.when((c < heads - 1) & jnp.logical_not(early))
        def _():
            gather_cross(c + 1)

        @pl.when(c > 0)
        def _():
            reduce_send(c - 1)

    repeat(0, heads, head)
    final = heads - 1
    reduce_side(final)
    if heads > 1:
        reduce_final(final - 1)
    repeat(0, final - 1, spread_forward)
    reduce_send(final)
    x_forward()
    if heads > 1:
        spread_forward(final - 1)
    reduce_final(final)
    repeat(0, final, spread_cross)

    x_arrive()
    for i in range(count):
        xt[:, i * rows:(i + 1) * rows] = xc[i].T
    spread_forward(final)
    for d in range(1, mp_count):
        peer = lax.rem(mine + d, mp_count)
        weight_copy(peer, peer).wait_recv()
        for c in range(heads):
            pair_copy(c, peer, peer).wait_recv()

    contract = (((1,), (1,)), ((), ()))

    def input_term(c, m, block):
        return lax.dot_general(pair[m, c], block, contract, preferred_element_type=F32)

    own_rows = pl.ds(pl.multiple_of(mine * w_rows, w_rows), w_rows)
    for c in range(heads):
        cols = slice(c * HD, (c + 1) * HD)
        term = input_term(c, mine, w_ref[own_rows, cols])
        ig_acc[...] = term if c == 0 else ig_acc[...] + term
    spread_cross(final)
    for d in range(1, mp_count):
        peer = lax.rem(mine + d, mp_count)
        for c in range(heads):
            ig_acc[...] += input_term(c, peer, wr[peer, :, c * HD:(c + 1) * HD])
    ig_ref[...] = ig_acc[...].astype(BF)
    for c in range(heads):
        spread_arrive(c)
        wg_ref[:, c * HD:(c + 1) * HD] = dot(
            xt[...], all_v[c].reshape(count * rows, HD)
        ).astype(BF)

    for d in range(1, mp_count):
        peer = lax.rem(mine + d, mp_count)
        weight_copy(peer, mine).wait_send()
        for c in range(heads):
            pair_copy(c, peer, mine).wait_send()
    x_finish()
    repeat(0, heads, gather_finish)
    repeat(0, heads, reduce_finish)
    repeat(0, heads, spread_finish)


def hand_over(*refs):
    for i in range(4):
        refs[4 + i][...] = refs[i][...]


def on_device(
    sublayer_input, rotated_queries, rotated_keys, output_grad, value_weight,
    segment_ids, label_positions,
):
    rows, features = sublayer_input.shape
    count = lax.axis_size("ctx")
    mp_count = lax.axis_size("mp")
    slabs = count // SLAB
    total_rows = rows * count
    width = rotated_keys.shape[1]
    heads = width // HD
    span = GROUP * rows
    kb = 2 * rows
    x_cols = features // count
    x_split = x_cols % 128 != 0
    pieces = sublayer_input
    if x_split:
        pieces = sublayer_input.reshape(rows, count, x_cols).transpose(1, 0, 2)
    keep = total_rows <= 4096
    kept = (total_rows // kb, kb, span) if keep else (1, 8, 128)
    vmem = pl.BlockSpec(memory_space=pltpu.VMEM)
    dma = pltpu.SemaphoreType.DMA
    chunk = (rows, 2 * HD)
    pairs = rows * GROUP * heads * total_rows
    results = pl.pallas_call(
        functools.partial(kernel, count, mp_count, heads, keep, x_split),
        out_shape=(
            jax.ShapeDtypeStruct(rotated_queries.shape, BF),
            jax.ShapeDtypeStruct((rows, width), BF),
            jax.ShapeDtypeStruct((rows, features // mp_count), BF),
            jax.ShapeDtypeStruct((x_cols, width), BF),
        ),
        in_specs=[vmem] * 7,
        out_specs=(vmem,) * 4,
        scratch_shapes=[
            pltpu.VMEM((heads, count) + chunk, BF),
            pltpu.VMEM((heads, count) + chunk, BF),
            pltpu.VMEM((heads, 2, slabs) + chunk, BF),
            pltpu.VMEM((heads, slabs) + chunk, BF),
            pltpu.VMEM((heads, slabs) + chunk, BF),
            pltpu.VMEM((heads, slabs) + chunk, BF),
            pltpu.VMEM((heads, slabs) + chunk, BF),
            pltpu.VMEM((heads, count, rows, HD), BF),
            pltpu.VMEM((mp_count, heads, rows, HD), BF),
            pltpu.VMEM((count, rows, x_cols), BF),
            pltpu.VMEM((x_cols, total_rows), BF),
            pltpu.VMEM((mp_count, features // mp_count, width), BF),
            pltpu.VMEM((span, HD), BF),
            pltpu.VMEM((HD, span), BF),
            pltpu.VMEM((span, HD), BF),
            pltpu.VMEM((HD, span), BF),
            pltpu.VMEM((1, span), F32),
            pltpu.VMEM((1, span), F32),
            pltpu.VMEM((1, span), F32),
            pltpu.VMEM((HD, span), F32),
            pltpu.VMEM((kb, span), BF),
            pltpu.VMEM((kb, span), BF),
            pltpu.VMEM((total_rows // kb, 1, span), F32),
            pltpu.VMEM(kept, F32),
            pltpu.VMEM(kept, F32),
            pltpu.VMEM((rows, features // mp_count), F32),
            dma((heads, count)),
            dma((heads, 2, count)),
            dma((heads, slabs)),
            dma((heads, 2, slabs)),
            dma((heads, slabs)),
            dma((heads, slabs)),
            dma((heads, 2, slabs)),
            dma((heads, slabs)),
            dma((heads, slabs)),
            dma((heads, count)),
            dma((heads, 2, count)),
            dma((heads, slabs)),
            dma((heads, mp_count)),
            dma((heads, mp_count)),
            dma((count,)),
            dma((count,)),
            dma,
            dma((mp_count,)),
            dma((mp_count,)),
            dma((mp_count,)),
        ],
        compiler_params=pltpu.CompilerParams(
            collective_id=0, has_side_effects=True, vmem_limit_bytes=VMEM_LIMIT
        ),
        cost_estimate=pl.CostEstimate(
            flops=5 * pairs * HD, bytes_accessed=total_rows * width * 8, transcendentals=pairs
        ),
        name="attention_backward",
    )(segment_ids[None, :], label_positions[None, :], rotated_queries, output_grad,
      rotated_keys, pieces, value_weight)
    return pl.pallas_call(
        hand_over,
        out_shape=tuple(jax.ShapeDtypeStruct(r.shape, r.dtype) for r in results),
        in_specs=[vmem] * 4,
        out_specs=(vmem,) * 4,
        name="hand_over",
    )(*results)


def solution(mesh):
    placed = (
        P("ctx", None),
        P("ctx", "mp"),
        P("ctx", "mp"),
        P("ctx", "mp"),
        P(None, "mp"),
        P(),
        P(),
    )
    return jax.shard_map(
        on_device,
        mesh=mesh,
        in_specs=placed,
        out_specs=(P("ctx", "mp"), P("ctx", "mp"), P("ctx", "mp"), P("ctx", "mp")),
        check_vma=False,
    )
```

```python
import functools

import jax
import jax.numpy as jnp
from jax import lax
from jax.experimental import pallas as pl
from jax.experimental.pallas import tpu as pltpu
from jax.sharding import PartitionSpec as P

HEADS = 64
KV_HEADS = 8
HD = 128
GROUP = HEADS // KV_HEADS
SCALE = HD ** (-0.5)
LOG2E = 1.4426950408889634
NEGATIVE = -1e30
MESH = pl.DeviceIdType.MESH
SLAB = 4
CORE = 1
SIDE = 2
BF = jnp.bfloat16
F32 = jnp.float32
VMEM_LIMIT = 56 * 1024 * 1024


def remote(src, dst, send, recv, axis, index):
    return pltpu.make_async_remote_copy(
        src_ref=src,
        dst_ref=dst,
        send_sem=send,
        recv_sem=recv,
        device_id={axis: index},
        device_id_type=MESH,
    )


def flip(pos, bit):
    if bit == CORE:
        return pos + 1 - 2 * lax.rem(pos, 2)
    return lax.rem(pos + 2, SLAB)


def dot(a, b):
    return jnp.dot(a, b, preferred_element_type=F32)


def greet(me, count, mp_count):
    barrier = pltpu.get_barrier_semaphore()

    def along(d, _):
        peer = lax.rem(me + d, count)
        pl.semaphore_signal(barrier, inc=1, device_id={"ctx": peer}, device_id_type=MESH)
        return 0

    lax.fori_loop(1, count, along, 0)
    mine = lax.axis_index("mp")
    for d in range(1, mp_count):
        peer = lax.rem(mine + d, mp_count)
        pl.semaphore_signal(barrier, inc=1, device_id={"mp": peer}, device_id_type=MESH)
    return barrier


def repeat(low, high, body):
    def step(i, _):
        body(i)
        return 0

    lax.fori_loop(low, high, step, 0)


def kernel(
    count, mp_count, heads, keep, x_split,
    seg_ref, label_ref, q_ref, g_ref, k_ref, x_ref, w_ref,
    dq_ref, dk_ref, ig_ref, wg_ref,
    kv, part, rc, ry, rz, sy, sz, all_v, pair, xc, xt, wr,
    qs, qt, gs, gt, top, total, dotted, dq_acc, pb, sb, block_top, e_all, p_all, ig_acc,
    g_recv, g_send, gz_send, rc_sem, ry_sem, rz_sem, sc_sem, sy_sem, sz_sem,
    ag_recv, ag_send, agz_send, mp_recv, mp_send, x_recv, x_send, xf_recv, xf_send,
    w_recv, w_send,
):
    rows = q_ref.shape[0]
    wide = 2 * rows
    kb = 2 * rows
    slabs = count // SLAB
    me = lax.axis_index("ctx")
    mine = lax.axis_index("mp")
    slab = me // SLAB
    pos = lax.rem(me, SLAB)
    base = me - pos
    core_pos, side_pos = flip(pos, CORE), flip(pos, SIDE)
    both_pos = flip(side_pos, CORE)
    first_row = me * rows
    blocks = me // 2 + 1
    barrier = greet(me, count, mp_count)

    if x_split:
        values = jnp.zeros((rows, k_ref.shape[1]), F32)
        for t in range(count):
            values += dot(x_ref[t], w_ref[t * xc.shape[2]:(t + 1) * xc.shape[2], :])
    else:
        values = dot(x_ref[...], w_ref[...])
    values = values.astype(BF)
    position = first_row + lax.broadcasted_iota(jnp.int32, (rows, label_ref.shape[1]), 0)
    loss_weight = jnp.max(
        jnp.where(position == label_ref[...], 4.0, 1.0).astype(F32), axis=1, keepdims=True
    )
    segments = seg_ref[...]
    own_segments = seg_ref[:, pl.ds(pl.multiple_of(first_row, rows), rows)]
    begin = jnp.zeros((1, rows), jnp.int32)
    for v in range(1, 4):
        before = jnp.sum(jnp.where(segments < v, 1.0, 0.0), axis=1, keepdims=True)
        begin = jnp.where(own_segments == v, before.astype(jnp.int32), begin)
    pl.semaphore_wait(barrier, count - 1 + mp_count - 1)

    w_rows = w_ref.shape[0] // mp_count

    def weight_copy(peer, slot):
        at = pl.ds(pl.multiple_of(peer * w_rows, w_rows), w_rows)
        return remote(w_ref.at[at, :], wr.at[slot], w_send.at[peer], w_recv.at[slot], "mp", peer)

    def gather_copy(c, dest, block):
        target = (base + side_pos, base + core_pos)[dest]
        ref = kv.at[c, block]
        return remote(ref, ref, g_send.at[c, dest, block], g_recv.at[c, block], "ctx", target)

    def gather_up(c, t):
        ref = kv.at[c, me]
        return remote(ref, ref, gz_send.at[c, t], g_recv.at[c, me], "ctx", t * SLAB + pos)

    def gather_own(c):
        cols = pl.ds(pl.multiple_of(c * HD, HD), HD)
        kv[c, me, :, :HD] = k_ref[:, cols]
        repeat(slab + 1, slabs, lambda t: gather_up(c, t).start())
        gather_copy(c, 0, me).start()
        gather_copy(c, 1, me).start()

    def gather_forward(c):
        def one(k):
            block = (slab - k) * SLAB + pos
            gather_copy(c, 0, block).wait_recv()
            gather_copy(c, 0, block).start()
            gather_copy(c, 1, block).start()

        repeat(1, slab + 1, one)

    def gather_cross(c):
        def one(k):
            block = (slab - k) * SLAB + side_pos
            gather_copy(c, 0, block).wait_recv()
            gather_copy(c, 1, block).start()

        repeat(0, slab + 1, one)

    def gather_arrive(c):
        def one(s):
            gather_copy(c, 1, s * SLAB + core_pos).wait_recv()
            gather_copy(c, 1, s * SLAB + both_pos).wait_recv()

        repeat(0, slab + 1, one)

    def gather_finish(c):
        def one(s):
            gather_copy(c, 0, s * SLAB + pos).wait_send()
            gather_copy(c, 1, s * SLAB + pos).wait_send()
            gather_copy(c, 1, s * SLAB + side_pos).wait_send()

        repeat(0, slab + 1, one)
        repeat(slab + 1, slabs, lambda t: gather_up(c, t).wait_send())

    def core_copy(c, which, s):
        block = s * SLAB + (core_pos, both_pos)[which]
        return remote(
            part.at[c, block], rc.at[c, which, s],
            sc_sem.at[c, which, s], rc_sem.at[c, which, s], "ctx", base + core_pos,
        )

    def side_copy(c, s):
        return remote(
            sy.at[c, s], ry.at[c, s], sy_sem.at[c, s], ry_sem.at[c, s], "ctx", base + side_pos
        )

    def down_copy(c, s):
        return remote(
            sz.at[c, s], rz.at[c, slab], sz_sem.at[c, s], rz_sem.at[c, slab],
            "ctx", s * SLAB + pos,
        )

    def down_arrival(c, t):
        return remote(
            sz.at[c, t], rz.at[c, t], sz_sem.at[c, t], rz_sem.at[c, t], "ctx", base + core_pos
        )

    def reduce_core(c):
        def one(s):
            core_copy(c, 1, s).start()
            core_copy(c, 0, s).start()

        repeat(0, slab + 1, one)

    def reduce_side(c):
        def one(s):
            core_copy(c, 1, s).wait_recv()
            both = part[c, s * SLAB + side_pos].astype(F32) + rc[c, 1, s].astype(F32)
            sy[c, s] = both.astype(BF)
            side_copy(c, s).start()

        repeat(0, slab + 1, one)

    def slab_total(c, s):
        core_copy(c, 0, s).wait_recv()
        both = part[c, s * SLAB + pos].astype(F32) + rc[c, 0, s].astype(F32)
        side_copy(c, s).wait_recv()
        return both + ry[c, s].astype(F32)

    def reduce_send(c):
        def one(s):
            sz[c, s] = slab_total(c, s).astype(BF)
            down_copy(c, s).start()

        repeat(0, slab, one)

    def reduce_final(c):
        def one(t, full):
            down_arrival(c, t).wait_recv()
            return full + rz[c, t].astype(F32)

        low = lax.fori_loop(slab + 1, slabs, one, slab_total(c, slab)).astype(BF)
        dk_ref[:, pl.ds(pl.multiple_of(c * HD, HD), HD)] = low[:, :HD]
        all_v[c, me] = low[:, HD:]
        pair[mine, c] = low[:, HD:]
        repeat(1, slabs, lambda k: spread_far(c, k).start())
        spread_copy(c, 0, me).start()
        spread_copy(c, 1, me).start()
        for d in range(1, mp_count):
            pair_copy(c, lax.rem(mine + d, mp_count), mine).start()

    def reduce_finish(c):
        def one(s):
            core_copy(c, 0, s).wait_send()
            core_copy(c, 1, s).wait_send()
            side_copy(c, s).wait_send()

            @pl.when(s < slab)
            def _():
                down_copy(c, s).wait_send()

        repeat(0, slab + 1, one)

    def pair_copy(c, peer, slot):
        return remote(
            all_v.at[c, me], pair.at[slot, c], mp_send.at[c, peer], mp_recv.at[c, slot],
            "mp", peer,
        )

    def spread_copy(c, dest, block):
        target = (base + side_pos, base + core_pos)[dest]
        ref = all_v.at[c, block]
        return remote(ref, ref, ag_send.at[c, dest, block], ag_recv.at[c, block], "ctx", target)

    def spread_far(c, k):
        t = lax.rem(slab + k, slabs)
        ref = all_v.at[c, me]
        return remote(ref, ref, agz_send.at[c, t], ag_recv.at[c, me], "ctx", t * SLAB + pos)

    def spread_forward(c):
        def one(k):
            block = lax.rem(slab + k, slabs) * SLAB + pos
            spread_copy(c, 0, block).wait_recv()
            spread_copy(c, 0, block).start()
            spread_copy(c, 1, block).start()

        repeat(1, slabs, one)

    def spread_cross(c):
        def one(k):
            block = lax.rem(slab + k, slabs) * SLAB + side_pos
            spread_copy(c, 0, block).wait_recv()
            spread_copy(c, 1, block).start()

        repeat(0, slabs, one)

    def spread_arrive(c):
        def one(s):
            spread_copy(c, 1, s * SLAB + core_pos).wait_recv()
            spread_copy(c, 1, s * SLAB + both_pos).wait_recv()

        repeat(0, slabs, one)

    def spread_finish(c):
        def one(s):
            spread_copy(c, 0, s * SLAB + pos).wait_send()
            spread_copy(c, 1, s * SLAB + pos).wait_send()
            spread_copy(c, 1, s * SLAB + side_pos).wait_send()

        repeat(0, slabs, one)
        repeat(1, slabs, lambda k: spread_far(c, k).wait_send())

    owner = lax.rem(me, mp_count) == mine
    x_cols = xc.shape[2]

    def x_piece(t):
        if x_split:
            return x_ref.at[t]
        return x_ref.at[:, pl.ds(pl.multiple_of(t * x_cols, x_cols), x_cols)]

    def x_copy(t, slot):
        return remote(x_piece(t), xc.at[slot], x_send.at[t], x_recv.at[slot], "ctx", t)

    def x_start():
        @pl.when(owner)
        def _():
            xc[me] = x_piece(me)[...]

        def one(i):
            t = lax.rem(i * mp_count + mine + (me // mp_count) * mp_count, count)

            @pl.when(t != me)
            def _():
                x_copy(t, me).start()

        repeat(0, count // mp_count, one)

    def x_over(peer):
        return remote(xc, xc, xf_send.at[peer], xf_recv, "mp", peer)

    def x_forward():
        @pl.when(owner)
        def _():
            def one(d):
                peer = lax.rem(me + d, count)
                x_copy(peer, peer).wait_recv()

            repeat(1, count, one)
            for d in range(1, mp_count):
                x_over(lax.rem(mine + d, mp_count)).start()

    def x_arrive():
        if mp_count > 1:
            @pl.when(jnp.logical_not(owner))
            def _():
                x_over(lax.rem(mine + 1, mp_count)).wait_recv()

    def x_finish():
        def one(i):
            t = i * mp_count + mine

            @pl.when(t != me)
            def _():
                x_copy(t, me).wait_send()

        repeat(0, count // mp_count, one)

        @pl.when(owner)
        def _():
            for d in range(1, mp_count):
                x_over(lax.rem(mine + d, mp_count)).wait_send()

    row_at = first_row + lax.broadcasted_iota(jnp.int32, (1, rows), 1)

    def visible(j):
        at = j * kb + lax.broadcasted_iota(jnp.int32, (kb, rows), 0)
        seen = (at >= begin) & (at <= row_at)
        return jnp.concatenate([seen, seen], axis=1)

    def key_block(c, j):
        return kv[c, pl.ds(2 * j, 2), :, :HD].reshape(kb, HD)

    def value_block(c, j):
        return kv[c, pl.ds(2 * j, 2), :, HD:].reshape(kb, HD)

    def terms(c, j, seen, span):
        scores = dot(key_block(c, j), qt[:, span]) * (SCALE * LOG2E)
        return jnp.where(seen, scores, NEGATIVE), dot(value_block(c, j), gt[:, span])

    def prepare(c):
        for g in range(GROUP):
            cols = pl.ds(pl.multiple_of((c * GROUP + g) * HD, HD), HD)
            span = slice(g * rows, (g + 1) * rows)
            q = q_ref[:, cols]
            grad = (g_ref[:, cols].astype(F32) * loss_weight).astype(BF)
            qs[span, :] = q
            gs[span, :] = grad
            qt[:, span] = q.T
            gt[:, span] = grad.T
        dq_acc[...] = jnp.zeros_like(dq_acc)
        top[...] = jnp.full_like(top, NEGATIVE)
        total[...] = jnp.zeros_like(total)
        dotted[...] = jnp.zeros_like(dotted)

    def first_pass(c):
        def one(j):
            seen = visible(j)
            for tile in range(GROUP // 2):
                span = slice(tile * wide, (tile + 1) * wide)
                scores, grad_probs = terms(c, j, seen, span)
                old = top[:, span]
                new = jnp.maximum(old, jnp.max(scores, axis=0, keepdims=True))
                e = jnp.exp2(scores - new)
                factor = jnp.exp2(old - new)
                top[:, span] = new
                total[:, span] = total[:, span] * factor + jnp.sum(e, axis=0, keepdims=True)
                dotted[:, span] = dotted[:, span] * factor + jnp.sum(
                    e * grad_probs, axis=0, keepdims=True
                )
                if keep:
                    block_top[j, :, span] = new
                    e_all[j, :, span] = e
                    p_all[j, :, span] = grad_probs

        repeat(0, blocks, one)
        total[...] = 1.0 / total[...]
        dotted[...] = dotted[...] * total[...]

    def second_pass(c):
        for i in range(SLAB):
            part[c, base + i] = jnp.zeros((rows, 2 * HD), BF)

        def one(j):
            if not keep:
                seen = visible(j)
            for tile in range(GROUP // 2):
                span = slice(tile * wide, (tile + 1) * wide)
                if keep:
                    ratio = jnp.exp2(block_top[j, :, span] - top[:, span]) * total[:, span]
                    probs = e_all[j, :, span] * ratio
                    grad_probs = p_all[j, :, span]
                else:
                    scores, grad_probs = terms(c, j, seen, span)
                    probs = jnp.exp2(scores - top[:, span]) * total[:, span]
                pb[:, span] = probs.astype(BF)
                sb[:, span] = (probs * (grad_probs - dotted[:, span])).astype(BF)
            low = sb[...]
            at = pl.ds(2 * j, 2)
            value_term = dot(pb[...], gs[...]).astype(BF)
            key_term = (dot(low, qs[...]) * SCALE).astype(BF)
            part[c, at, :, HD:] = value_term.reshape(2, rows, HD)
            part[c, at, :, :HD] = key_term.reshape(2, rows, HD)
            dq_acc[...] += dot(key_block(c, j).T, low)

        repeat(0, blocks, one)
        for g in range(GROUP):
            cols = pl.ds(pl.multiple_of((c * GROUP + g) * HD, HD), HD)
            dq_ref[:, cols] = (dq_acc[:, g * rows:(g + 1) * rows] * SCALE).T.astype(BF)

    for c in range(heads):
        kv[c, me, :, HD:] = values[:, c * HD:(c + 1) * HD]
    early = slab < slabs // 2
    gather_own(0)
    gather_forward(0)
    gather_cross(0)
    for d in range(1, mp_count):
        weight_copy(lax.rem(mine + d, mp_count), mine).start()
    if heads > 1:
        gather_own(1)

    def gather_early(c):
        gather_forward(c)

        @pl.when(c < heads - 1)
        def _():
            gather_own(c + 1)

        gather_cross(c)

    repeat(1, jnp.where(early, heads, 1), gather_early)

    def head(c):
        prepare(c)
        gather_arrive(c)

        @pl.when(c == min(1, heads - 1))
        def _():
            x_start()

        first_pass(c)

        @pl.when((c < heads - 1) & jnp.logical_not(early))
        def _():
            gather_forward(c + 1)

            @pl.when(c < heads - 2)
            def _():
                gather_own(c + 2)

        @pl.when(c > 0)
        def _():
            reduce_side(c - 1)

        @pl.when(c > 1)
        def _():
            reduce_final(c - 2)

        @pl.when(c == heads - 1)
        def _():
            x_forward()

        second_pass(c)
        reduce_core(c)

        @pl.when((c < heads - 1) & jnp.logical_not(early))
        def _():
            gather_cross(c + 1)

        @pl.when(c > 0)
        def _():
            reduce_send(c - 1)

        @pl.when(c > 1)
        def _():
            spread_forward(c - 2)

    repeat(0, heads, head)
    final = heads - 1
    reduce_side(final)
    if heads > 1:
        reduce_final(final - 1)
    repeat(0, final - 1, spread_cross)
    reduce_send(final)
    if heads > 1:
        spread_forward(final - 1)

    contract = (((1,), (1,)), ((), ()))
    own_rows = pl.ds(pl.multiple_of(mine * w_rows, w_rows), w_rows)

    def input_terms(c):
        cols = slice(c * HD, (c + 1) * HD)

        def term(m, block):
            return lax.dot_general(pair[m, c], block, contract, preferred_element_type=F32)

        found = term(mine, w_ref[own_rows, cols])
        ig_acc[...] = found if c == 0 else ig_acc[...] + found
        for d in range(1, mp_count):
            peer = lax.rem(mine + d, mp_count)
            pair_copy(c, peer, peer).wait_recv()
            ig_acc[...] += term(peer, wr[peer, :, cols])

    def weight_term(c):
        spread_arrive(c)
        wg_ref[:, c * HD:(c + 1) * HD] = dot(
            xt[...], all_v[c].reshape(count * rows, HD)
        ).astype(BF)

    x_arrive()
    for i in range(count):
        xt[:, i * rows:(i + 1) * rows] = xc[i].T
    for d in range(1, mp_count):
        peer = lax.rem(mine + d, mp_count)
        weight_copy(peer, peer).wait_recv()
    for c in range(final - 1):
        weight_term(c)
    reduce_final(final)
    if heads > 1:
        spread_cross(final - 1)
    for c in range(final):
        input_terms(c)
    spread_forward(final)
    input_terms(final)
    spread_cross(final)
    ig_ref[...] = ig_acc[...].astype(BF)
    for c in range(max(final - 1, 0), heads):
        weight_term(c)

    for d in range(1, mp_count):
        peer = lax.rem(mine + d, mp_count)
        weight_copy(peer, mine).wait_send()
        for c in range(heads):
            pair_copy(c, peer, mine).wait_send()
    x_finish()
    repeat(0, heads, gather_finish)
    repeat(0, heads, reduce_finish)
    repeat(0, heads, spread_finish)


def hand_over(*refs):
    for i in range(4):
        refs[4 + i][...] = refs[i][...]


def on_device(
    sublayer_input, rotated_queries, rotated_keys, output_grad, value_weight,
    segment_ids, label_positions,
):
    rows, features = sublayer_input.shape
    count = lax.axis_size("ctx")
    mp_count = lax.axis_size("mp")
    slabs = count // SLAB
    total_rows = rows * count
    width = rotated_keys.shape[1]
    heads = width // HD
    span = GROUP * rows
    kb = 2 * rows
    x_cols = features // count
    x_split = x_cols % 128 != 0
    pieces = sublayer_input
    if x_split:
        pieces = sublayer_input.reshape(rows, count, x_cols).transpose(1, 0, 2)
    keep = total_rows <= 4096
    kept = (total_rows // kb, kb, span) if keep else (1, 8, 128)
    vmem = pl.BlockSpec(memory_space=pltpu.VMEM)
    dma = pltpu.SemaphoreType.DMA
    chunk = (rows, 2 * HD)
    pairs = rows * GROUP * heads * total_rows
    results = pl.pallas_call(
        functools.partial(kernel, count, mp_count, heads, keep, x_split),
        out_shape=(
            jax.ShapeDtypeStruct(rotated_queries.shape, BF),
            jax.ShapeDtypeStruct((rows, width), BF),
            jax.ShapeDtypeStruct((rows, features // mp_count), BF),
            jax.ShapeDtypeStruct((x_cols, width), BF),
        ),
        in_specs=[vmem] * 7,
        out_specs=(vmem,) * 4,
        scratch_shapes=[
            pltpu.VMEM((heads, count) + chunk, BF),
            pltpu.VMEM((heads, count) + chunk, BF),
            pltpu.VMEM((heads, 2, slabs) + chunk, BF),
            pltpu.VMEM((heads, slabs) + chunk, BF),
            pltpu.VMEM((heads, slabs) + chunk, BF),
            pltpu.VMEM((heads, slabs) + chunk, BF),
            pltpu.VMEM((heads, slabs) + chunk, BF),
            pltpu.VMEM((heads, count, rows, HD), BF),
            pltpu.VMEM((mp_count, heads, rows, HD), BF),
            pltpu.VMEM((count, rows, x_cols), BF),
            pltpu.VMEM((x_cols, total_rows), BF),
            pltpu.VMEM((mp_count, features // mp_count, width), BF),
            pltpu.VMEM((span, HD), BF),
            pltpu.VMEM((HD, span), BF),
            pltpu.VMEM((span, HD), BF),
            pltpu.VMEM((HD, span), BF),
            pltpu.VMEM((1, span), F32),
            pltpu.VMEM((1, span), F32),
            pltpu.VMEM((1, span), F32),
            pltpu.VMEM((HD, span), F32),
            pltpu.VMEM((kb, span), BF),
            pltpu.VMEM((kb, span), BF),
            pltpu.VMEM((total_rows // kb, 1, span), F32),
            pltpu.VMEM(kept, F32),
            pltpu.VMEM(kept, F32),
            pltpu.VMEM((rows, features // mp_count), F32),
            dma((heads, count)),
            dma((heads, 2, count)),
            dma((heads, slabs)),
            dma((heads, 2, slabs)),
            dma((heads, slabs)),
            dma((heads, slabs)),
            dma((heads, 2, slabs)),
            dma((heads, slabs)),
            dma((heads, slabs)),
            dma((heads, count)),
            dma((heads, 2, count)),
            dma((heads, slabs)),
            dma((heads, mp_count)),
            dma((heads, mp_count)),
            dma((count,)),
            dma((count,)),
            dma,
            dma((mp_count,)),
            dma((mp_count,)),
            dma((mp_count,)),
        ],
        compiler_params=pltpu.CompilerParams(
            collective_id=0, has_side_effects=True, vmem_limit_bytes=VMEM_LIMIT
        ),
        cost_estimate=pl.CostEstimate(
            flops=5 * pairs * HD, bytes_accessed=total_rows * width * 8, transcendentals=pairs
        ),
        name="attention_backward",
    )(segment_ids[None, :], label_positions[None, :], rotated_queries, output_grad,
      rotated_keys, pieces, value_weight)
    return pl.pallas_call(
        hand_over,
        out_shape=tuple(jax.ShapeDtypeStruct(r.shape, r.dtype) for r in results),
        in_specs=[vmem] * 4,
        out_specs=(vmem,) * 4,
        name="hand_over",
    )(*results)


def solution(mesh):
    placed = (
        P("ctx", None),
        P("ctx", "mp"),
        P("ctx", "mp"),
        P("ctx", "mp"),
        P(None, "mp"),
        P(),
        P(),
    )
    return jax.shard_map(
        on_device,
        mesh=mesh,
        in_specs=placed,
        out_specs=(P("ctx", "mp"), P("ctx", "mp"), P("ctx", "mp"), P("ctx", "mp")),
        check_vma=False,
    )
```

```python
import functools

import jax
import jax.numpy as jnp
from jax import lax
from jax.experimental import pallas as pl
from jax.experimental.pallas import tpu as pltpu
from jax.sharding import PartitionSpec as P

HEADS = 64
KV_HEADS = 8
HD = 128
GROUP = HEADS // KV_HEADS
SCALE = HD ** (-0.5)
LOG2E = 1.4426950408889634
NEGATIVE = -1e30
MESH = pl.DeviceIdType.MESH
SLAB = 4
CORE = 1
SIDE = 2
BF = jnp.bfloat16
F32 = jnp.float32
VMEM_LIMIT = 56 * 1024 * 1024


def remote(src, dst, send, recv, axis, index):
    return pltpu.make_async_remote_copy(
        src_ref=src,
        dst_ref=dst,
        send_sem=send,
        recv_sem=recv,
        device_id={axis: index},
        device_id_type=MESH,
    )


def flip(pos, bit):
    if bit == CORE:
        return pos + 1 - 2 * lax.rem(pos, 2)
    return lax.rem(pos + 2, SLAB)


def dot(a, b):
    return jnp.dot(a, b, preferred_element_type=F32)


def greet(me, count, mp_count):
    barrier = pltpu.get_barrier_semaphore()

    def along(d, _):
        peer = lax.rem(me + d, count)
        pl.semaphore_signal(barrier, inc=1, device_id={"ctx": peer}, device_id_type=MESH)
        return 0

    lax.fori_loop(1, count, along, 0)
    mine = lax.axis_index("mp")
    for d in range(1, mp_count):
        peer = lax.rem(mine + d, mp_count)
        pl.semaphore_signal(barrier, inc=1, device_id={"mp": peer}, device_id_type=MESH)
    return barrier


def repeat(low, high, body):
    def step(i, _):
        body(i)
        return 0

    lax.fori_loop(low, high, step, 0)


def kernel(
    count, mp_count, heads, keep, x_split,
    seg_ref, label_ref, q_ref, g_ref, k_ref, x_ref, w_ref,
    dq_ref, dk_ref, ig_ref, wg_ref,
    kv, part, rc, ry, rz, sy, sz, all_v, pair, xc, xt, wr,
    qs, qt, gs, gt, top, total, dotted, dq_acc, pb, sb, block_top, e_all, p_all, ig_acc,
    gz_recv, gz_send, gy_sem, gc_sem, rc_sem, ry_sem, rz_sem, sz_sem,
    az_recv, az_send, ay_sem, ac_sem, mp_recv, mp_send, x_recv, x_send, xf_recv, xf_send,
    w_recv, w_send,
):
    rows = q_ref.shape[0]
    wide = 2 * rows
    kb = 2 * rows
    slabs = count // SLAB
    me = lax.axis_index("ctx")
    mine = lax.axis_index("mp")
    slab = me // SLAB
    pos = lax.rem(me, SLAB)
    base = me - pos
    core, side = lax.rem(pos, 2), pos // 2
    core_mate, side_mate = base + flip(pos, CORE), base + flip(pos, SIDE)
    first_row = me * rows
    blocks = me // 2 + 1
    barrier = greet(me, count, mp_count)

    if x_split:
        values = jnp.zeros((rows, k_ref.shape[1]), F32)
        for t in range(count):
            values += dot(x_ref[t], w_ref[t * xc.shape[2]:(t + 1) * xc.shape[2], :])
    else:
        values = dot(x_ref[...], w_ref[...])
    values = values.astype(BF)
    position = first_row + lax.broadcasted_iota(jnp.int32, (rows, label_ref.shape[1]), 0)
    loss_weight = jnp.max(
        jnp.where(position == label_ref[...], 4.0, 1.0).astype(F32), axis=1, keepdims=True
    )
    segments = seg_ref[...]
    own_segments = seg_ref[:, pl.ds(pl.multiple_of(first_row, rows), rows)]
    begin = jnp.zeros((1, rows), jnp.int32)
    for v in range(1, 4):
        before = jnp.sum(jnp.where(segments < v, 1.0, 0.0), axis=1, keepdims=True)
        begin = jnp.where(own_segments == v, before.astype(jnp.int32), begin)
    pl.semaphore_wait(barrier, count - 1 + mp_count - 1)

    w_rows = w_ref.shape[0] // mp_count

    def weight_copy(peer, slot):
        at = pl.ds(pl.multiple_of(peer * w_rows, w_rows), w_rows)
        return remote(w_ref.at[at, :], wr.at[slot], w_send.at[peer], w_recv.at[slot], "mp", peer)

    def gather_up(c, t):
        ref = kv.at[c, core, side, slab]
        return remote(
            ref, ref, gz_send.at[c, t], gz_recv.at[c, slab], "ctx", t * SLAB + pos
        )

    def gather_below(c, t):
        ref = kv.at[c, core, side, t]
        return remote(ref, ref, gz_send.at[c, t], gz_recv.at[c, t], "ctx", core_mate)

    def gather_side(c, column):
        ref = kv.at[c, core, column]
        return remote(ref, ref, gy_sem.at[c, 0], gy_sem.at[c, 1], "ctx", side_mate)

    def gather_core(c, half):
        ref = kv.at[c, half]
        return remote(ref, ref, gc_sem.at[c, 0], gc_sem.at[c, 1], "ctx", core_mate)

    def gather_own(c):
        cols = pl.ds(pl.multiple_of(c * HD, HD), HD)
        kv[c, core, side, slab, :, :HD] = k_ref[:, cols]
        repeat(slab + 1, slabs, lambda t: gather_up(c, t).start())

    def gather_forward(c):
        repeat(0, slab, lambda t: gather_below(c, t).wait_recv())
        gather_side(c, side).start()

    def gather_cross(c):
        gather_side(c, 1 - side).wait_recv()
        gather_core(c, core).start()

    def gather_arrive(c):
        gather_core(c, 1 - core).wait_recv()

    def gather_finish(c):
        gather_side(c, side).wait_send()
        gather_core(c, core).wait_send()
        repeat(slab + 1, slabs, lambda t: gather_up(c, t).wait_send())

    def core_copy(c):
        return remote(
            part.at[c, 1 - core], rc.at[c], rc_sem.at[c, 0], rc_sem.at[c, 1], "ctx", core_mate
        )

    def side_copy(c):
        return remote(
            sy.at[c], ry.at[c], ry_sem.at[c, 0], ry_sem.at[c, 1], "ctx", side_mate
        )

    def down_copy(c, s):
        return remote(
            sz.at[c, s], rz.at[c, slab], sz_sem.at[c, s], rz_sem.at[c, slab],
            "ctx", s * SLAB + pos,
        )

    def down_arrival(c, t):
        return remote(
            sz.at[c, t], rz.at[c, t], sz_sem.at[c, t], rz_sem.at[c, t], "ctx", core_mate
        )

    def reduce_core(c):
        core_copy(c).start()

    def reduce_side(c):
        core_copy(c).wait_recv()

        def one(s):
            both = part[c, core, 1 - side, s].astype(F32) + rc[c, 1 - side, s].astype(F32)
            sy[c, s] = both.astype(BF)

        repeat(0, slab + 1, one)
        side_copy(c).start()

    def slab_total(c, s):
        both = part[c, core, side, s].astype(F32) + rc[c, side, s].astype(F32)
        return both + ry[c, s].astype(F32)

    def reduce_send(c):
        side_copy(c).wait_recv()

        def one(s):
            sz[c, s] = slab_total(c, s).astype(BF)
            down_copy(c, s).start()

        repeat(0, slab, one)

    def reduce_final(c):
        def one(t, full):
            down_arrival(c, t).wait_recv()
            return full + rz[c, t].astype(F32)

        low = lax.fori_loop(slab + 1, slabs, one, slab_total(c, slab)).astype(BF)
        dk_ref[:, pl.ds(pl.multiple_of(c * HD, HD), HD)] = low[:, :HD]
        all_v[c, core, side, slab] = low[:, HD:]
        pair[mine, c] = low[:, HD:]
        repeat(1, slabs, lambda k: spread_far(c, k).start())
        for d in range(1, mp_count):
            pair_copy(c, lax.rem(mine + d, mp_count), mine).start()

    def reduce_finish(c):
        core_copy(c).wait_send()
        side_copy(c).wait_send()
        repeat(0, slab, lambda t: down_copy(c, t).wait_send())

    def pair_copy(c, peer, slot):
        return remote(
            all_v.at[c, core, side, slab], pair.at[slot, c], mp_send.at[c, peer], mp_recv.at[c, slot],
            "mp", peer,
        )

    def spread_far(c, k):
        t = lax.rem(slab + k, slabs)
        ref = all_v.at[c, core, side, slab]
        return remote(
            ref, ref, az_send.at[c, t], az_recv.at[c, slab], "ctx", t * SLAB + pos
        )

    def spread_near(c, k):
        t = lax.rem(slab + k, slabs)
        ref = all_v.at[c, core, side, t]
        return remote(ref, ref, az_send.at[c, t], az_recv.at[c, t], "ctx", core_mate)

    def spread_side(c, column):
        ref = all_v.at[c, core, column]
        return remote(ref, ref, ay_sem.at[c, 0], ay_sem.at[c, 1], "ctx", side_mate)

    def spread_core(c, half):
        ref = all_v.at[c, half]
        return remote(ref, ref, ac_sem.at[c, 0], ac_sem.at[c, 1], "ctx", core_mate)

    def spread_forward(c):
        repeat(1, slabs, lambda k: spread_near(c, k).wait_recv())
        spread_side(c, side).start()

    def spread_cross(c):
        spread_side(c, 1 - side).wait_recv()
        spread_core(c, core).start()

    def spread_arrive(c):
        spread_core(c, 1 - core).wait_recv()

    def spread_finish(c):
        spread_side(c, side).wait_send()
        spread_core(c, core).wait_send()
        repeat(1, slabs, lambda k: spread_far(c, k).wait_send())

    owner = lax.rem(me, mp_count) == mine
    x_cols = xc.shape[2]

    def x_piece(t):
        if x_split:
            return x_ref.at[t]
        return x_ref.at[:, pl.ds(pl.multiple_of(t * x_cols, x_cols), x_cols)]

    def x_copy(t, slot):
        return remote(x_piece(t), xc.at[slot], x_send.at[t], x_recv.at[slot], "ctx", t)

    def x_start():
        @pl.when(owner)
        def _():
            xc[me] = x_piece(me)[...]

        def one(i):
            t = lax.rem(i * mp_count + mine + (me // mp_count) * mp_count, count)

            @pl.when(t != me)
            def _():
                x_copy(t, me).start()

        repeat(0, count // mp_count, one)

    def x_over(peer):
        return remote(xc, xc, xf_send.at[peer], xf_recv, "mp", peer)

    def x_forward():
        @pl.when(owner)
        def _():
            def one(d):
                peer = lax.rem(me + d, count)
                x_copy(peer, peer).wait_recv()

            repeat(1, count, one)
            for d in range(1, mp_count):
                x_over(lax.rem(mine + d, mp_count)).start()

    def x_arrive():
        if mp_count > 1:
            @pl.when(jnp.logical_not(owner))
            def _():
                x_over(lax.rem(mine + 1, mp_count)).wait_recv()

    def x_finish():
        def one(i):
            t = i * mp_count + mine

            @pl.when(t != me)
            def _():
                x_copy(t, me).wait_send()

        repeat(0, count // mp_count, one)

        @pl.when(owner)
        def _():
            for d in range(1, mp_count):
                x_over(lax.rem(mine + d, mp_count)).wait_send()

    row_at = first_row + lax.broadcasted_iota(jnp.int32, (1, rows), 1)

    def visible(j):
        at = j * kb + lax.broadcasted_iota(jnp.int32, (kb, rows), 0)
        seen = (at >= begin) & (at <= row_at)
        return jnp.concatenate([seen, seen], axis=1)

    def key_block(c, j):
        return kv[c, :, lax.rem(j, 2), j // 2, :, :HD].reshape(kb, HD)

    def value_block(c, j):
        return kv[c, :, lax.rem(j, 2), j // 2, :, HD:].reshape(kb, HD)

    def terms(c, j, seen, span):
        scores = dot(key_block(c, j), qt[:, span]) * (SCALE * LOG2E)
        return jnp.where(seen, scores, NEGATIVE), dot(value_block(c, j), gt[:, span])

    def prepare(c):
        for g in range(GROUP):
            cols = pl.ds(pl.multiple_of((c * GROUP + g) * HD, HD), HD)
            span = slice(g * rows, (g + 1) * rows)
            q = q_ref[:, cols]
            grad = (g_ref[:, cols].astype(F32) * loss_weight).astype(BF)
            qs[span, :] = q
            gs[span, :] = grad
            qt[:, span] = q.T
            gt[:, span] = grad.T
        dq_acc[...] = jnp.zeros_like(dq_acc)
        top[...] = jnp.full_like(top, NEGATIVE)
        total[...] = jnp.zeros_like(total)
        dotted[...] = jnp.zeros_like(dotted)

    def first_pass(c):
        def one(j):
            seen = visible(j)
            for tile in range(GROUP // 2):
                span = slice(tile * wide, (tile + 1) * wide)
                scores, grad_probs = terms(c, j, seen, span)
                old = top[:, span]
                new = jnp.maximum(old, jnp.max(scores, axis=0, keepdims=True))
                e = jnp.exp2(scores - new)
                factor = jnp.exp2(old - new)
                top[:, span] = new
                total[:, span] = total[:, span] * factor + jnp.sum(e, axis=0, keepdims=True)
                dotted[:, span] = dotted[:, span] * factor + jnp.sum(
                    e * grad_probs, axis=0, keepdims=True
                )
                if keep:
                    block_top[j, :, span] = new
                    e_all[j, :, span] = e
                    p_all[j, :, span] = grad_probs

        repeat(0, blocks, one)
        total[...] = 1.0 / total[...]
        dotted[...] = dotted[...] * total[...]

    def second_pass(c):
        for i in range(SLAB):
            part[c, i // 2, i % 2, slab] = jnp.zeros((rows, 2 * HD), BF)

        def one(j):
            if not keep:
                seen = visible(j)
            for tile in range(GROUP // 2):
                span = slice(tile * wide, (tile + 1) * wide)
                if keep:
                    ratio = jnp.exp2(block_top[j, :, span] - top[:, span]) * total[:, span]
                    probs = e_all[j, :, span] * ratio
                    grad_probs = p_all[j, :, span]
                else:
                    scores, grad_probs = terms(c, j, seen, span)
                    probs = jnp.exp2(scores - top[:, span]) * total[:, span]
                pb[:, span] = probs.astype(BF)
                sb[:, span] = (probs * (grad_probs - dotted[:, span])).astype(BF)
            low = sb[...]
            column, at = lax.rem(j, 2), j // 2
            value_term = dot(pb[...], gs[...]).astype(BF)
            key_term = (dot(low, qs[...]) * SCALE).astype(BF)
            part[c, :, column, at, :, HD:] = value_term.reshape(2, rows, HD)
            part[c, :, column, at, :, :HD] = key_term.reshape(2, rows, HD)
            dq_acc[...] += dot(key_block(c, j).T, low)

        repeat(0, blocks, one)
        for g in range(GROUP):
            cols = pl.ds(pl.multiple_of((c * GROUP + g) * HD, HD), HD)
            dq_ref[:, cols] = (dq_acc[:, g * rows:(g + 1) * rows] * SCALE).T.astype(BF)

    for c in range(heads):
        kv[c, core, side, slab, :, HD:] = values[:, c * HD:(c + 1) * HD]
    early = slab < slabs // 2
    gather_own(0)
    gather_forward(0)
    gather_cross(0)
    for d in range(1, mp_count):
        weight_copy(lax.rem(mine + d, mp_count), mine).start()
    if heads > 1:
        gather_own(1)

    def gather_early(c):
        gather_forward(c)

        @pl.when(c < heads - 1)
        def _():
            gather_own(c + 1)

        gather_cross(c)

    repeat(1, jnp.where(early, heads, 1), gather_early)

    def head(c):
        prepare(c)
        gather_arrive(c)

        @pl.when(c == min(1, heads - 1))
        def _():
            x_start()

        first_pass(c)

        @pl.when((c < heads - 1) & jnp.logical_not(early))
        def _():
            gather_forward(c + 1)

            @pl.when(c < heads - 2)
            def _():
                gather_own(c + 2)

        @pl.when(c > 0)
        def _():
            reduce_side(c - 1)

        @pl.when(c > 1)
        def _():
            reduce_final(c - 2)

        @pl.when(c == heads - 1)
        def _():
            x_forward()

        second_pass(c)
        reduce_core(c)

        @pl.when((c < heads - 1) & jnp.logical_not(early))
        def _():
            gather_cross(c + 1)

        @pl.when(c > 0)
        def _():
            reduce_send(c - 1)

        @pl.when(c > 1)
        def _():
            spread_forward(c - 2)

    repeat(0, heads, head)
    final = heads - 1
    reduce_side(final)
    if heads > 1:
        reduce_final(final - 1)
    repeat(0, final - 1, spread_cross)
    reduce_send(final)
    if heads > 1:
        spread_forward(final - 1)

    contract = (((1,), (1,)), ((), ()))
    own_rows = pl.ds(pl.multiple_of(mine * w_rows, w_rows), w_rows)

    def input_terms(c):
        cols = slice(c * HD, (c + 1) * HD)

        def term(m, block):
            return lax.dot_general(pair[m, c], block, contract, preferred_element_type=F32)

        found = term(mine, w_ref[own_rows, cols])
        ig_acc[...] = found if c == 0 else ig_acc[...] + found
        for d in range(1, mp_count):
            peer = lax.rem(mine + d, mp_count)
            pair_copy(c, peer, peer).wait_recv()
            ig_acc[...] += term(peer, wr[peer, :, cols])

    def weight_term(c):
        spread_arrive(c)
        wg_ref[:, c * HD:(c + 1) * HD] = dot(
            xt[...], all_v[c].reshape(count * rows, HD)
        ).astype(BF)

    x_arrive()
    for i in range(count):
        at = (i % 2 * 2 + i % SLAB // 2) * slabs + i // SLAB
        xt[:, at * rows:(at + 1) * rows] = xc[i].T
    for d in range(1, mp_count):
        peer = lax.rem(mine + d, mp_count)
        weight_copy(peer, peer).wait_recv()
    for c in range(final - 1):
        weight_term(c)
    reduce_final(final)
    if heads > 1:
        spread_cross(final - 1)
    for c in range(final):
        input_terms(c)
    spread_forward(final)
    input_terms(final)
    spread_cross(final)
    ig_ref[...] = ig_acc[...].astype(BF)
    for c in range(max(final - 1, 0), heads):
        weight_term(c)

    for d in range(1, mp_count):
        peer = lax.rem(mine + d, mp_count)
        weight_copy(peer, mine).wait_send()
        for c in range(heads):
            pair_copy(c, peer, mine).wait_send()
    x_finish()
    repeat(0, heads, gather_finish)
    repeat(0, heads, reduce_finish)
    repeat(0, heads, spread_finish)


def hand_over(*refs):
    for i in range(4):
        refs[4 + i][...] = refs[i][...]


def on_device(
    sublayer_input, rotated_queries, rotated_keys, output_grad, value_weight,
    segment_ids, label_positions,
):
    rows, features = sublayer_input.shape
    count = lax.axis_size("ctx")
    mp_count = lax.axis_size("mp")
    slabs = count // SLAB
    total_rows = rows * count
    width = rotated_keys.shape[1]
    heads = width // HD
    span = GROUP * rows
    kb = 2 * rows
    x_cols = features // count
    x_split = x_cols % 128 != 0
    pieces = sublayer_input
    if x_split:
        pieces = sublayer_input.reshape(rows, count, x_cols).transpose(1, 0, 2)
    keep = total_rows <= 4096
    kept = (total_rows // kb, kb, span) if keep else (1, 8, 128)
    vmem = pl.BlockSpec(memory_space=pltpu.VMEM)
    dma = pltpu.SemaphoreType.DMA
    chunk = (rows, 2 * HD)
    pairs = rows * GROUP * heads * total_rows
    results = pl.pallas_call(
        functools.partial(kernel, count, mp_count, heads, keep, x_split),
        out_shape=(
            jax.ShapeDtypeStruct(rotated_queries.shape, BF),
            jax.ShapeDtypeStruct((rows, width), BF),
            jax.ShapeDtypeStruct((rows, features // mp_count), BF),
            jax.ShapeDtypeStruct((x_cols, width), BF),
        ),
        in_specs=[vmem] * 7,
        out_specs=(vmem,) * 4,
        scratch_shapes=[
            pltpu.VMEM((heads, 2, 2, slabs) + chunk, BF),
            pltpu.VMEM((heads, 2, 2, slabs) + chunk, BF),
            pltpu.VMEM((heads, 2, slabs) + chunk, BF),
            pltpu.VMEM((heads, slabs) + chunk, BF),
            pltpu.VMEM((heads, slabs) + chunk, BF),
            pltpu.VMEM((heads, slabs) + chunk, BF),
            pltpu.VMEM((heads, slabs) + chunk, BF),
            pltpu.VMEM((heads, 2, 2, slabs, rows, HD), BF),
            pltpu.VMEM((mp_count, heads, rows, HD), BF),
            pltpu.VMEM((count, rows, x_cols), BF),
            pltpu.VMEM((x_cols, total_rows), BF),
            pltpu.VMEM((mp_count, features // mp_count, width), BF),
            pltpu.VMEM((span, HD), BF),
            pltpu.VMEM((HD, span), BF),
            pltpu.VMEM((span, HD), BF),
            pltpu.VMEM((HD, span), BF),
            pltpu.VMEM((1, span), F32),
            pltpu.VMEM((1, span), F32),
            pltpu.VMEM((1, span), F32),
            pltpu.VMEM((HD, span), F32),
            pltpu.VMEM((kb, span), BF),
            pltpu.VMEM((kb, span), BF),
            pltpu.VMEM((total_rows // kb, 1, span), F32),
            pltpu.VMEM(kept, F32),
            pltpu.VMEM(kept, F32),
            pltpu.VMEM((rows, features // mp_count), F32),
            dma((heads, slabs)),
            dma((heads, slabs)),
            dma((heads, 2)),
            dma((heads, 2)),
            dma((heads, 2)),
            dma((heads, 2)),
            dma((heads, slabs)),
            dma((heads, slabs)),
            dma((heads, slabs)),
            dma((heads, slabs)),
            dma((heads, 2)),
            dma((heads, 2)),
            dma((heads, mp_count)),
            dma((heads, mp_count)),
            dma((count,)),
            dma((count,)),
            dma,
            dma((mp_count,)),
            dma((mp_count,)),
            dma((mp_count,)),
        ],
        compiler_params=pltpu.CompilerParams(
            collective_id=0, has_side_effects=True, vmem_limit_bytes=VMEM_LIMIT
        ),
        cost_estimate=pl.CostEstimate(
            flops=5 * pairs * HD, bytes_accessed=total_rows * width * 8, transcendentals=pairs
        ),
        name="attention_backward",
    )(segment_ids[None, :], label_positions[None, :], rotated_queries, output_grad,
      rotated_keys, pieces, value_weight)
    return pl.pallas_call(
        hand_over,
        out_shape=tuple(jax.ShapeDtypeStruct(r.shape, r.dtype) for r in results),
        in_specs=[vmem] * 4,
        out_specs=(vmem,) * 4,
        name="hand_over",
    )(*results)


def solution(mesh):
    placed = (
        P("ctx", None),
        P("ctx", "mp"),
        P("ctx", "mp"),
        P("ctx", "mp"),
        P(None, "mp"),
        P(),
        P(),
    )
    return jax.shard_map(
        on_device,
        mesh=mesh,
        in_specs=placed,
        out_specs=(P("ctx", "mp"), P("ctx", "mp"), P("ctx", "mp"), P("ctx", "mp")),
        check_vma=False,
    )
```

```python
import functools

import jax
import jax.numpy as jnp
from jax import lax
from jax.experimental import pallas as pl
from jax.experimental.pallas import tpu as pltpu
from jax.sharding import PartitionSpec as P

HEADS = 64
KV_HEADS = 8
HD = 128
GROUP = HEADS // KV_HEADS
SCALE = HD ** (-0.5)
LOG2E = 1.4426950408889634
NEGATIVE = -1e30
MESH = pl.DeviceIdType.MESH
SLAB = 4
CORE = 1
SIDE = 2
BF = jnp.bfloat16
F32 = jnp.float32
VMEM_LIMIT = 56 * 1024 * 1024


def remote(src, dst, send, recv, axis, index):
    return pltpu.make_async_remote_copy(
        src_ref=src,
        dst_ref=dst,
        send_sem=send,
        recv_sem=recv,
        device_id={axis: index},
        device_id_type=MESH,
    )


def flip(pos, bit):
    if bit == CORE:
        return pos + 1 - 2 * lax.rem(pos, 2)
    return lax.rem(pos + 2, SLAB)


def dot(a, b):
    return jnp.dot(a, b, preferred_element_type=F32)


def greet(me, count, mp_count):
    barrier = pltpu.get_barrier_semaphore()

    def along(d, _):
        peer = lax.rem(me + d, count)
        pl.semaphore_signal(barrier, inc=1, device_id={"ctx": peer}, device_id_type=MESH)
        return 0

    lax.fori_loop(1, count, along, 0)
    mine = lax.axis_index("mp")
    for d in range(1, mp_count):
        peer = lax.rem(mine + d, mp_count)
        pl.semaphore_signal(barrier, inc=1, device_id={"mp": peer}, device_id_type=MESH)
    return barrier


def repeat(low, high, body):
    def step(i, _):
        body(i)
        return 0

    lax.fori_loop(low, high, step, 0)


def kernel(
    count, mp_count, heads, keep, x_split,
    seg_ref, label_ref, q_ref, g_ref, k_ref, x_ref, w_ref,
    dq_ref, dk_ref, ig_ref, wg_ref,
    kv, part, rc, ry, rz, sy, sz, all_v, pair, xc, xt, wr,
    qs, qt, gs, gt, top, total, dotted, dq_acc, pb, sb, block_top, e_all, p_all, ig_acc,
    g_recv, g_send, gz_send, rc_sem, ry_sem, rz_sem, sc_sem, sy_sem, sz_sem,
    ag_recv, ag_send, agz_send, mp_recv, mp_send, x_recv, x_send, xf_recv, xf_send,
    w_recv, w_send,
):
    rows = q_ref.shape[0]
    wide = 2 * rows
    kb = 2 * rows
    slabs = count // SLAB
    me = lax.axis_index("ctx")
    mine = lax.axis_index("mp")
    slab = me // SLAB
    pos = lax.rem(me, SLAB)
    base = me - pos
    core_pos, side_pos = flip(pos, CORE), flip(pos, SIDE)
    both_pos = flip(side_pos, CORE)
    first_row = me * rows
    blocks = me // 2 + 1
    barrier = greet(me, count, mp_count)

    if x_split:
        values = jnp.zeros((rows, k_ref.shape[1]), F32)
        for t in range(count):
            values += dot(x_ref[t], w_ref[t * xc.shape[2]:(t + 1) * xc.shape[2], :])
    else:
        values = dot(x_ref[...], w_ref[...])
    values = values.astype(BF)
    position = first_row + lax.broadcasted_iota(jnp.int32, (rows, label_ref.shape[1]), 0)
    loss_weight = jnp.max(
        jnp.where(position == label_ref[...], 4.0, 1.0).astype(F32), axis=1, keepdims=True
    )
    segments = seg_ref[...]
    own_segments = seg_ref[:, pl.ds(pl.multiple_of(first_row, rows), rows)]
    begin = jnp.zeros((1, rows), jnp.int32)
    for v in range(1, 4):
        before = jnp.sum(jnp.where(segments < v, 1.0, 0.0), axis=1, keepdims=True)
        begin = jnp.where(own_segments == v, before.astype(jnp.int32), begin)
    pl.semaphore_wait(barrier, count - 1 + mp_count - 1)

    w_rows = w_ref.shape[0] // mp_count

    def weight_copy(peer, slot):
        at = pl.ds(pl.multiple_of(peer * w_rows, w_rows), w_rows)
        return remote(w_ref.at[at, :], wr.at[slot], w_send.at[peer], w_recv.at[slot], "mp", peer)

    def gather_copy(c, dest, block):
        target = (base + side_pos, base + core_pos)[dest]
        ref = kv.at[c, block]
        return remote(ref, ref, g_send.at[c, dest, block], g_recv.at[c, block], "ctx", target)

    def gather_up(c, t):
        ref = kv.at[c, me]
        return remote(ref, ref, gz_send.at[c, t], g_recv.at[c, me], "ctx", t * SLAB + pos)

    def gather_own(c):
        cols = pl.ds(pl.multiple_of(c * HD, HD), HD)
        kv[c, me, :, :HD] = k_ref[:, cols]
        repeat(slab + 1, slabs, lambda t: gather_up(c, t).start())
        gather_copy(c, 0, me).start()
        gather_copy(c, 1, me).start()

    def gather_forward(c):
        def one(k):
            block = (slab - k) * SLAB + pos
            gather_copy(c, 0, block).wait_recv()
            gather_copy(c, 0, block).start()
            gather_copy(c, 1, block).start()

        repeat(1, slab + 1, one)

    def gather_cross(c):
        def one(k):
            block = (slab - k) * SLAB + side_pos
            gather_copy(c, 0, block).wait_recv()
            gather_copy(c, 1, block).start()

        repeat(0, slab + 1, one)

    def gather_arrive(c):
        def one(s):
            gather_copy(c, 1, s * SLAB + core_pos).wait_recv()
            gather_copy(c, 1, s * SLAB + both_pos).wait_recv()

        repeat(0, slab + 1, one)

    def gather_finish(c):
        def one(s):
            gather_copy(c, 0, s * SLAB + pos).wait_send()
            gather_copy(c, 1, s * SLAB + pos).wait_send()
            gather_copy(c, 1, s * SLAB + side_pos).wait_send()

        repeat(0, slab + 1, one)
        repeat(slab + 1, slabs, lambda t: gather_up(c, t).wait_send())

    def core_copy(c, which, s):
        block = s * SLAB + (core_pos, both_pos)[which]
        return remote(
            part.at[c, block], rc.at[c, which, s],
            sc_sem.at[c, which, s], rc_sem.at[c, which, s], "ctx", base + core_pos,
        )

    def side_copy(c, s):
        return remote(
            sy.at[c, s], ry.at[c, s], sy_sem.at[c, s], ry_sem.at[c, s], "ctx", base + side_pos
        )

    def down_copy(c, s):
        return remote(
            sz.at[c, s], rz.at[c, slab], sz_sem.at[c, s], rz_sem.at[c, slab],
            "ctx", s * SLAB + pos,
        )

    def down_arrival(c, t):
        return remote(
            sz.at[c, t], rz.at[c, t], sz_sem.at[c, t], rz_sem.at[c, t], "ctx", base + core_pos
        )

    def reduce_core(c):
        def one(s):
            core_copy(c, 1, s).start()
            core_copy(c, 0, s).start()

        repeat(0, slab + 1, one)

    def reduce_side(c):
        def one(s):
            core_copy(c, 1, s).wait_recv()
            both = part[c, s * SLAB + side_pos].astype(F32) + rc[c, 1, s].astype(F32)
            sy[c, s] = both.astype(BF)
            side_copy(c, s).start()

        repeat(0, slab + 1, one)

    def slab_total(c, s):
        core_copy(c, 0, s).wait_recv()
        both = part[c, s * SLAB + pos].astype(F32) + rc[c, 0, s].astype(F32)
        side_copy(c, s).wait_recv()
        return both + ry[c, s].astype(F32)

    def reduce_send(c):
        def one(s):
            sz[c, s] = slab_total(c, s).astype(BF)
            down_copy(c, s).start()

        repeat(0, slab, one)

    def reduce_final(c):
        def one(t, full):
            down_arrival(c, t).wait_recv()
            return full + rz[c, t].astype(F32)

        low = lax.fori_loop(slab + 1, slabs, one, slab_total(c, slab)).astype(BF)
        dk_ref[:, pl.ds(pl.multiple_of(c * HD, HD), HD)] = low[:, :HD]
        all_v[c, me] = low[:, HD:]
        pair[mine, c] = low[:, HD:]
        repeat(1, slabs, lambda k: spread_far(c, k).start())
        spread_copy(c, 0, me).start()
        spread_copy(c, 1, me).start()
        for d in range(1, mp_count):
            pair_copy(c, lax.rem(mine + d, mp_count), mine).start()

    def reduce_finish(c):
        def one(s):
            core_copy(c, 0, s).wait_send()
            core_copy(c, 1, s).wait_send()
            side_copy(c, s).wait_send()

            @pl.when(s < slab)
            def _():
                down_copy(c, s).wait_send()

        repeat(0, slab + 1, one)

    def pair_copy(c, peer, slot):
        return remote(
            all_v.at[c, me], pair.at[slot, c], mp_send.at[c, peer], mp_recv.at[c, slot],
            "mp", peer,
        )

    def spread_copy(c, dest, block):
        target = (base + side_pos, base + core_pos)[dest]
        ref = all_v.at[c, block]
        return remote(ref, ref, ag_send.at[c, dest, block], ag_recv.at[c, block], "ctx", target)

    def spread_far(c, k):
        t = lax.rem(slab + k, slabs)
        ref = all_v.at[c, me]
        return remote(ref, ref, agz_send.at[c, t], ag_recv.at[c, me], "ctx", t * SLAB + pos)

    def spread_forward(c):
        def one(k):
            block = lax.rem(slab + k, slabs) * SLAB + pos
            spread_copy(c, 0, block).wait_recv()
            spread_copy(c, 0, block).start()
            spread_copy(c, 1, block).start()

        repeat(1, slabs, one)

    def spread_cross(c):
        def one(k):
            block = lax.rem(slab + k, slabs) * SLAB + side_pos
            spread_copy(c, 0, block).wait_recv()
            spread_copy(c, 1, block).start()

        repeat(0, slabs, one)

    def spread_arrive(c):
        def one(s):
            spread_copy(c, 1, s * SLAB + core_pos).wait_recv()
            spread_copy(c, 1, s * SLAB + both_pos).wait_recv()

        repeat(0, slabs, one)

    def spread_finish(c):
        def one(s):
            spread_copy(c, 0, s * SLAB + pos).wait_send()
            spread_copy(c, 1, s * SLAB + pos).wait_send()
            spread_copy(c, 1, s * SLAB + side_pos).wait_send()

        repeat(0, slabs, one)
        repeat(1, slabs, lambda k: spread_far(c, k).wait_send())

    owner = lax.rem(me, mp_count) == mine
    x_cols = xc.shape[2]

    def x_piece(t):
        if x_split:
            return x_ref.at[t]
        return x_ref.at[:, pl.ds(pl.multiple_of(t * x_cols, x_cols), x_cols)]

    def x_copy(t, slot):
        return remote(x_piece(t), xc.at[slot], x_send.at[t], x_recv.at[slot], "ctx", t)

    def x_start():
        @pl.when(owner)
        def _():
            xc[me] = x_piece(me)[...]

        def one(i):
            t = lax.rem(i * mp_count + mine + (me // mp_count) * mp_count, count)

            @pl.when(t != me)
            def _():
                x_copy(t, me).start()

        repeat(0, count // mp_count, one)

    def x_over(peer):
        return remote(xc, xc, xf_send.at[peer], xf_recv, "mp", peer)

    def x_forward():
        @pl.when(owner)
        def _():
            def one(d):
                peer = lax.rem(me + d, count)
                x_copy(peer, peer).wait_recv()

            repeat(1, count, one)
            for d in range(1, mp_count):
                x_over(lax.rem(mine + d, mp_count)).start()

    def x_arrive():
        if mp_count > 1:
            @pl.when(jnp.logical_not(owner))
            def _():
                x_over(lax.rem(mine + 1, mp_count)).wait_recv()

    def x_finish():
        def one(i):
            t = i * mp_count + mine

            @pl.when(t != me)
            def _():
                x_copy(t, me).wait_send()

        repeat(0, count // mp_count, one)

        @pl.when(owner)
        def _():
            for d in range(1, mp_count):
                x_over(lax.rem(mine + d, mp_count)).wait_send()

    row_at = first_row + lax.broadcasted_iota(jnp.int32, (1, rows), 1)

    def visible(j):
        at = j * kb + lax.broadcasted_iota(jnp.int32, (kb, rows), 0)
        seen = (at >= begin) & (at <= row_at)
        return jnp.concatenate([seen, seen], axis=1)

    def key_block(c, j):
        return kv[c, pl.ds(2 * j, 2), :, :HD].reshape(kb, HD)

    def value_block(c, j):
        return kv[c, pl.ds(2 * j, 2), :, HD:].reshape(kb, HD)

    def terms(c, j, seen, span):
        scores = dot(key_block(c, j), qt[:, span]) * (SCALE * LOG2E)
        return jnp.where(seen, scores, NEGATIVE), dot(value_block(c, j), gt[:, span])

    def prepare(c):
        for g in range(GROUP):
            cols = pl.ds(pl.multiple_of((c * GROUP + g) * HD, HD), HD)
            span = slice(g * rows, (g + 1) * rows)
            q = q_ref[:, cols]
            grad = (g_ref[:, cols].astype(F32) * loss_weight).astype(BF)
            qs[span, :] = q
            gs[span, :] = grad
            qt[:, span] = q.T
            gt[:, span] = grad.T
        dq_acc[...] = jnp.zeros_like(dq_acc)
        top[...] = jnp.full_like(top, NEGATIVE)
        total[...] = jnp.zeros_like(total)
        dotted[...] = jnp.zeros_like(dotted)

    def first_pass(c):
        def one(j):
            seen = visible(j)
            for tile in range(GROUP // 2):
                span = slice(tile * wide, (tile + 1) * wide)
                scores, grad_probs = terms(c, j, seen, span)
                old = top[:, span]
                new = jnp.maximum(old, jnp.max(scores, axis=0, keepdims=True))
                e = jnp.exp2(scores - new)
                factor = jnp.exp2(old - new)
                top[:, span] = new
                total[:, span] = total[:, span] * factor + jnp.sum(e, axis=0, keepdims=True)
                dotted[:, span] = dotted[:, span] * factor + jnp.sum(
                    e * grad_probs, axis=0, keepdims=True
                )
                if keep:
                    block_top[j, :, span] = new
                    e_all[j, :, span] = e
                    p_all[j, :, span] = grad_probs

        repeat(0, blocks, one)
        total[...] = 1.0 / total[...]
        dotted[...] = dotted[...] * total[...]

    def second_pass(c):
        for i in range(SLAB):
            part[c, base + i] = jnp.zeros((rows, 2 * HD), BF)

        def one(j):
            if not keep:
                seen = visible(j)
            for tile in range(GROUP // 2):
                span = slice(tile * wide, (tile + 1) * wide)
                if keep:
                    ratio = jnp.exp2(block_top[j, :, span] - top[:, span]) * total[:, span]
                    probs = e_all[j, :, span] * ratio
                    grad_probs = p_all[j, :, span]
                else:
                    scores, grad_probs = terms(c, j, seen, span)
                    probs = jnp.exp2(scores - top[:, span]) * total[:, span]
                pb[:, span] = probs.astype(BF)
                sb[:, span] = (probs * (grad_probs - dotted[:, span])).astype(BF)
            low = sb[...]
            at = pl.ds(2 * j, 2)
            value_term = dot(pb[...], gs[...]).astype(BF)
            key_term = (dot(low, qs[...]) * SCALE).astype(BF)
            part[c, at, :, HD:] = value_term.reshape(2, rows, HD)
            part[c, at, :, :HD] = key_term.reshape(2, rows, HD)
            dq_acc[...] += dot(key_block(c, j).T, low)

        repeat(0, blocks, one)
        for g in range(GROUP):
            cols = pl.ds(pl.multiple_of((c * GROUP + g) * HD, HD), HD)
            dq_ref[:, cols] = (dq_acc[:, g * rows:(g + 1) * rows] * SCALE).T.astype(BF)

    for c in range(heads):
        kv[c, me, :, HD:] = values[:, c * HD:(c + 1) * HD]
    early = slab < slabs // 2
    gather_own(0)
    gather_forward(0)
    if heads > 1:
        gather_own(1)
    gather_cross(0)
    for d in range(1, mp_count):
        weight_copy(lax.rem(mine + d, mp_count), mine).start()

    @pl.when(jnp.logical_not(early) & (heads > 2))
    def _():
        gather_own(min(2, heads - 1))

    def gather_early(c):
        gather_forward(c)

        @pl.when(c < heads - 1)
        def _():
            gather_own(c + 1)

        gather_cross(c)

    repeat(1, jnp.where(early, heads, 1), gather_early)

    late = jnp.logical_not(early)

    def head(c):
        prepare(c)
        gather_arrive(c)

        @pl.when(late & (c == 0) & (heads > 1))
        def _():
            gather_forward(min(1, heads - 1))

        @pl.when(c > 0)
        def _():
            reduce_side(c - 1)

        @pl.when(c == min(2, heads - 1))
        def _():
            x_start()

        first_pass(c)

        @pl.when(late & (c < heads - 2))
        def _():
            gather_forward(c + 2)

            @pl.when(c < heads - 3)
            def _():
                gather_own(c + 3)

        @pl.when(c > 1)
        def _():
            reduce_final(c - 2)

        @pl.when(c == heads - 1)
        def _():
            x_forward()

        second_pass(c)
        reduce_core(c)

        @pl.when((c < heads - 1) & jnp.logical_not(early))
        def _():
            gather_cross(c + 1)

        @pl.when(c > 0)
        def _():
            reduce_send(c - 1)

        @pl.when(c > 1)
        def _():
            spread_forward(c - 2)

    repeat(0, heads, head)
    final = heads - 1
    reduce_side(final)
    if heads > 1:
        reduce_final(final - 1)
    repeat(0, final - 1, spread_cross)
    reduce_send(final)
    if heads > 1:
        spread_forward(final - 1)

    contract = (((1,), (1,)), ((), ()))
    own_rows = pl.ds(pl.multiple_of(mine * w_rows, w_rows), w_rows)

    def input_terms(c):
        cols = slice(c * HD, (c + 1) * HD)

        def term(m, block):
            return lax.dot_general(pair[m, c], block, contract, preferred_element_type=F32)

        found = term(mine, w_ref[own_rows, cols])
        ig_acc[...] = found if c == 0 else ig_acc[...] + found
        for d in range(1, mp_count):
            peer = lax.rem(mine + d, mp_count)
            pair_copy(c, peer, peer).wait_recv()
            ig_acc[...] += term(peer, wr[peer, :, cols])

    def weight_term(c):
        spread_arrive(c)
        wg_ref[:, c * HD:(c + 1) * HD] = dot(
            xt[...], all_v[c].reshape(count * rows, HD)
        ).astype(BF)

    x_arrive()
    for i in range(count):
        xt[:, i * rows:(i + 1) * rows] = xc[i].T
    for d in range(1, mp_count):
        peer = lax.rem(mine + d, mp_count)
        weight_copy(peer, peer).wait_recv()
    for c in range(final - 1):
        weight_term(c)
    reduce_final(final)
    if heads > 1:
        spread_cross(final - 1)
    for c in range(final):
        input_terms(c)
    spread_forward(final)
    input_terms(final)
    spread_cross(final)
    ig_ref[...] = ig_acc[...].astype(BF)
    for c in range(max(final - 1, 0), heads):
        weight_term(c)

    for d in range(1, mp_count):
        peer = lax.rem(mine + d, mp_count)
        weight_copy(peer, mine).wait_send()
        for c in range(heads):
            pair_copy(c, peer, mine).wait_send()
    x_finish()
    repeat(0, heads, gather_finish)
    repeat(0, heads, reduce_finish)
    repeat(0, heads, spread_finish)


def hand_over(*refs):
    for i in range(4):
        refs[4 + i][...] = refs[i][...]


def on_device(
    sublayer_input, rotated_queries, rotated_keys, output_grad, value_weight,
    segment_ids, label_positions,
):
    rows, features = sublayer_input.shape
    count = lax.axis_size("ctx")
    mp_count = lax.axis_size("mp")
    slabs = count // SLAB
    total_rows = rows * count
    width = rotated_keys.shape[1]
    heads = width // HD
    span = GROUP * rows
    kb = 2 * rows
    x_cols = features // count
    x_split = x_cols % 128 != 0
    pieces = sublayer_input
    if x_split:
        pieces = sublayer_input.reshape(rows, count, x_cols).transpose(1, 0, 2)
    keep = total_rows <= 4096
    kept = (total_rows // kb, kb, span) if keep else (1, 8, 128)
    vmem = pl.BlockSpec(memory_space=pltpu.VMEM)
    dma = pltpu.SemaphoreType.DMA
    chunk = (rows, 2 * HD)
    pairs = rows * GROUP * heads * total_rows
    results = pl.pallas_call(
        functools.partial(kernel, count, mp_count, heads, keep, x_split),
        out_shape=(
            jax.ShapeDtypeStruct(rotated_queries.shape, BF),
            jax.ShapeDtypeStruct((rows, width), BF),
            jax.ShapeDtypeStruct((rows, features // mp_count), BF),
            jax.ShapeDtypeStruct((x_cols, width), BF),
        ),
        in_specs=[vmem] * 7,
        out_specs=(vmem,) * 4,
        scratch_shapes=[
            pltpu.VMEM((heads, count) + chunk, BF),
            pltpu.VMEM((heads, count) + chunk, BF),
            pltpu.VMEM((heads, 2, slabs) + chunk, BF),
            pltpu.VMEM((heads, slabs) + chunk, BF),
            pltpu.VMEM((heads, slabs) + chunk, BF),
            pltpu.VMEM((heads, slabs) + chunk, BF),
            pltpu.VMEM((heads, slabs) + chunk, BF),
            pltpu.VMEM((heads, count, rows, HD), BF),
            pltpu.VMEM((mp_count, heads, rows, HD), BF),
            pltpu.VMEM((count, rows, x_cols), BF),
            pltpu.VMEM((x_cols, total_rows), BF),
            pltpu.VMEM((mp_count, features // mp_count, width), BF),
            pltpu.VMEM((span, HD), BF),
            pltpu.VMEM((HD, span), BF),
            pltpu.VMEM((span, HD), BF),
            pltpu.VMEM((HD, span), BF),
            pltpu.VMEM((1, span), F32),
            pltpu.VMEM((1, span), F32),
            pltpu.VMEM((1, span), F32),
            pltpu.VMEM((HD, span), F32),
            pltpu.VMEM((kb, span), BF),
            pltpu.VMEM((kb, span), BF),
            pltpu.VMEM((total_rows // kb, 1, span), F32),
            pltpu.VMEM(kept, F32),
            pltpu.VMEM(kept, F32),
            pltpu.VMEM((rows, features // mp_count), F32),
            dma((heads, count)),
            dma((heads, 2, count)),
            dma((heads, slabs)),
            dma((heads, 2, slabs)),
            dma((heads, slabs)),
            dma((heads, slabs)),
            dma((heads, 2, slabs)),
            dma((heads, slabs)),
            dma((heads, slabs)),
            dma((heads, count)),
            dma((heads, 2, count)),
            dma((heads, slabs)),
            dma((heads, mp_count)),
            dma((heads, mp_count)),
            dma((count,)),
            dma((count,)),
            dma,
            dma((mp_count,)),
            dma((mp_count,)),
            dma((mp_count,)),
        ],
        compiler_params=pltpu.CompilerParams(
            collective_id=0, has_side_effects=True, vmem_limit_bytes=VMEM_LIMIT
        ),
        cost_estimate=pl.CostEstimate(
            flops=5 * pairs * HD, bytes_accessed=total_rows * width * 8, transcendentals=pairs
        ),
        name="attention_backward",
    )(segment_ids[None, :], label_positions[None, :], rotated_queries, output_grad,
      rotated_keys, pieces, value_weight)
    return pl.pallas_call(
        hand_over,
        out_shape=tuple(jax.ShapeDtypeStruct(r.shape, r.dtype) for r in results),
        in_specs=[vmem] * 4,
        out_specs=(vmem,) * 4,
        name="hand_over",
    )(*results)


def solution(mesh):
    placed = (
        P("ctx", None),
        P("ctx", "mp"),
        P("ctx", "mp"),
        P("ctx", "mp"),
        P(None, "mp"),
        P(),
        P(),
    )
    return jax.shard_map(
        on_device,
        mesh=mesh,
        in_specs=placed,
        out_specs=(P("ctx", "mp"), P("ctx", "mp"), P("ctx", "mp"), P("ctx", "mp")),
        check_vma=False,
    )
```
